32 devices in a mesh: seq: 8 (over y, x, core), chan: 4 (over z).
Axes of the slice: x: 2, y: 2, z: 4, core: 2. Of those that a mesh axis runs over, the one named last changes fastest.
Arguments:
- query_proj: bfloat16 [4096, 1024], P('chan', 'seq'), may hold values from -6 to 6
- key_proj: bfloat16 [4096, 1024], P('chan', 'seq'), may hold values from -6 to 6
- value_proj: bfloat16 [4096, 1024], P('chan', 'seq'), may hold values from -6 to 6
- cotangent: bfloat16 [4096, 1024], P('chan', 'seq'), may hold values from -6 to 6
- filter_taps: bfloat16 [1024, 1024], P('seq'), may hold values from -6 to 6
Outputs:
- gated_out: bfloat16 [4096, 1024], P('chan', 'seq')
- query_grad: bfloat16 [4096, 1024], P('chan', 'seq')
- key_grad: bfloat16 [4096, 1024], P('chan', 'seq')
- value_grad: bfloat16 [4096, 1024], P('chan', 'seq')
- filter_grad: float32 [1024, 1024], P('seq', 'chan')
The draws below stay inside these ranges and needn't reach their ends.
All inputs are finite; a program needn't handle non-finite values.
Results may differ from the reference program's by a relative error of at most 0.0057.
Values may be sent and summed in bfloat16 or wider, within the bound.
No kernel may reach another device: no remote copies, remote signals or barrier semaphores. Data moves between devices by JAX's collectives and lax.ppermute only.
A program may use at most 64 MiB of HBM per device.

```python
import math
import jax
import jax.numpy as jnp
from jax import lax

D = 4096
LEN = 1024
NF = 1024
N_CHAN = 4


def shard_levels(stream_key, dims, pieces, low, high):
    factor_of = 1.0
    for axis_at, parts in pieces:
        draws = jax.random.uniform(jax.random.fold_in(jax.random.fold_in(stream_key, 6), axis_at), (parts,), jnp.float32, low / len(pieces), high / len(pieces))
        factor_of = factor_of * jnp.repeat(jnp.exp(draws), dims[axis_at] // parts).reshape((-1,) + (1,) * (len(dims) - 1 - axis_at))
    return factor_of


def centred(rng, extent, scale, reach, pieces=(), kind=jnp.bfloat16):
    result = jax.random.normal(rng, extent, jnp.float32) * scale
    if len(pieces) > 0:
        result = shard_levels(rng, extent, pieces, -0.22, 0.18) * result
    return jnp.clip(result, min=-reach, max=reach).astype(kind)


def setup_inputs(seed: int = 0) -> dict:
    streams_of = jax.random.split(jax.random.key(seed), 6)
    return {
        "query_proj": centred(streams_of[0], (D, LEN), 1.0, 6.0, ((0, 4), (1, 8))),
        "key_proj": centred(streams_of[1], (D, LEN), 1.0, 6.0, ((0, 4), (1, 8))),
        "value_proj": centred(streams_of[2], (D, LEN), 1.0, 6.0, ((0, 4), (1, 8))),
        "cotangent": centred(streams_of[3], (D, LEN), 1.0, 6.0, ((0, 4), (1, 8))),
        "filter_taps": centred(streams_of[4], (NF, LEN), 1.0, 6.0, ((0, 8),)),
    }


def reference(query_proj, key_proj, value_proj, cotangent, filter_taps):
    scale = 1.0 / math.sqrt(LEN)
    taps = filter_taps.astype(jnp.float32) * scale
    filt_spec = jnp.fft.fft(taps, n=2 * LEN, axis=1)

    def block(index):
        start = (index * NF).astype(jnp.int32)
        query = lax.dynamic_slice_in_dim(query_proj, start, NF, 0).astype(jnp.float32)
        keyset = lax.dynamic_slice_in_dim(key_proj, start, NF, 0).astype(jnp.float32)
        values = lax.dynamic_slice_in_dim(value_proj, start, NF, 0).astype(jnp.float32)
        upstream = lax.dynamic_slice_in_dim(cotangent, start, NF, 0).astype(jnp.float32)
        mixed = (keyset * values).astype(jnp.bfloat16)
        pulled = (upstream * query).astype(jnp.bfloat16)
        mix_spec = jnp.fft.fft(mixed.astype(jnp.float32), n=2 * LEN, axis=1)
        pull_spec = jnp.fft.fft(pulled.astype(jnp.float32), n=2 * LEN, axis=1)
        conv = jnp.fft.ifft(mix_spec * filt_spec, axis=1).real[:, :LEN].astype(jnp.bfloat16)
        back = jnp.fft.ifft(pull_spec * jnp.conj(filt_spec), axis=1).real[:, :LEN].astype(jnp.bfloat16)
        lag = jnp.fft.ifft(pull_spec * jnp.conj(mix_spec), axis=1).real[:, :LEN] * scale
        conv_wide = conv.astype(jnp.float32)
        back_wide = back.astype(jnp.float32)
        gated = (query * conv_wide).astype(jnp.bfloat16)
        qgrad = (upstream * conv_wide).astype(jnp.bfloat16)
        kgrad = (back_wide * values).astype(jnp.bfloat16)
        vgrad = (back_wide * keyset).astype(jnp.bfloat16)
        return (gated, qgrad, kgrad, vgrad, lag.astype(jnp.float32))
    gated, qgrad, kgrad, vgrad, lags = lax.map(block, jnp.arange(N_CHAN, dtype=jnp.int32))
    filter_grad = lax.optimization_barrier(jnp.sum(lags, axis=0))
    return (gated.reshape(D, LEN), qgrad.reshape(D, LEN), kgrad.reshape(D, LEN), vgrad.reshape(D, LEN), filter_grad)
```

```python
import math

import jax
import jax.numpy as jnp
import ml_dtypes
import numpy as np
from jax import lax
from jax.experimental import pallas as pl
from jax.experimental.pallas import tpu as pltpu
from jax.sharding import PartitionSpec as P

BLOCK = 256
LANES = 128


def transform_tables(scale):
    freq = np.arange(BLOCK) + 0.5
    freq = np.concatenate([freq[0::2], freq[1::2]])
    angle = 2.0 * np.pi * np.outer(np.arange(BLOCK), freq) / (2 * BLOCK)
    forward = np.concatenate([np.cos(angle), -np.sin(angle)], axis=1)
    inverse = np.concatenate([np.cos(angle).T, -np.sin(angle).T], axis=0) * (scale / BLOCK)
    high = forward.astype(ml_dtypes.bfloat16)
    low = (forward - high.astype(np.float64)).astype(ml_dtypes.bfloat16)
    return high, low, inverse.astype(ml_dtypes.bfloat16)


def dot(left, right):
    return jnp.dot(left, right, preferred_element_type=jnp.float32)


def total(terms):
    real, imag = terms[0]
    for more_real, more_imag in terms[1:]:
        real, imag = real + more_real, imag + more_imag
    return real, imag


def times(left, right):
    return left[0] * right[0] - left[1] * right[1], left[0] * right[1] + left[1] * right[0]


def times_conj(left, right):
    return left[0] * right[0] + left[1] * right[1], left[1] * right[0] - left[0] * right[1]


def conv_kernel(cols_ref, taps_ref, high_ref, low_ref, inv_ref, out_ref, lag_ref, spec, filt, prod):
    chans, length = taps_ref.shape
    count = length // BLOCK
    width = lag_ref.shape[2]
    per = BLOCK // LANES
    for a in range(count):
        signal = jnp.concatenate([cols_ref[per * a + u] for u in range(per)], axis=1)
        spec[a] = dot(signal, high_ref[...]) + dot(signal, low_ref[...])
        taps = taps_ref[:, a * BLOCK : (a + 1) * BLOCK]
        filt[a] = dot(taps, high_ref[...]) + dot(taps, low_ref[...])
    tile = 16 if chans % 16 == 0 else chans

    def products(row):
        rows, others = pl.ds(row, tile), pl.ds(chans + row, tile)
        for half in range(BLOCK // LANES):
            sign = 1.0 if half < BLOCK // LANES // 2 else -1.0
            re, im = pl.ds(half * LANES, LANES), pl.ds(BLOCK + half * LANES, LANES)
            mixed = [(spec[a, rows, re], spec[a, rows, im]) for a in range(count)]
            pulled = [(spec[a, others, re], spec[a, others, im]) for a in range(count)]
            taps = [(filt[a, rows, re], filt[a, rows, im]) for a in range(count)]

            def put(which, c, value):
                prod[which, c, rows, re] = value[0].astype(jnp.bfloat16)
                prod[which, c, rows, im] = value[1].astype(jnp.bfloat16)

            before = None
            for c in range(count):
                here = total([times(mixed[a], taps[c - a]) for a in range(c + 1)])
                put(0, c, here if c == 0 else (here[0] - sign * before[1], here[1] + sign * before[0]))
                before = here
            for which, other in ((1, taps), (2, mixed)):
                after = None
                for c in reversed(range(count)):
                    here = total([times_conj(pulled[a], other[a - c]) for a in range(c, count)])
                    put(which, c, here if after is None else (here[0] + sign * after[1], here[1] - sign * after[0]))
                    after = here

    if chans == tile:
        products(0)
    else:

        def step(i, carry):
            products(pl.multiple_of(i * tile, tile))
            return carry

        lax.fori_loop(0, chans // tile, step, 0)
    for c in range(count):
        for which in range(3):
            result = dot(prod[which, c], inv_ref[...])
            for u in range(per):
                part = result[:, u * LANES : (u + 1) * LANES]
                at = per * c + u
                if which < 2:
                    out_ref[at, which * chans : (which + 1) * chans] = part.astype(jnp.bfloat16)
                else:
                    begin = at * LANES
                    lag_ref[begin // width, :, begin % width : begin % width + LANES] = part.astype(lag_ref.dtype)


def convolve(cols, taps, pieces):
    chans, length = taps.shape
    count = length // BLOCK
    high, low, inverse = transform_tables(1.0 / math.sqrt(length))
    vmem = pl.BlockSpec(memory_space=pltpu.VMEM)
    return pl.pallas_call(
        conv_kernel,
        out_shape=(
            jax.ShapeDtypeStruct(cols.shape, jnp.bfloat16),
            jax.ShapeDtypeStruct((pieces, chans, length // pieces), jnp.bfloat16),
        ),
        in_specs=[vmem] * 5,
        out_specs=(vmem, vmem),
        scratch_shapes=[
            pltpu.VMEM((count, 2 * chans, 2 * BLOCK), jnp.float32),
            pltpu.VMEM((count, chans, 2 * BLOCK), jnp.float32),
            pltpu.VMEM((3, count, chans, 2 * BLOCK), jnp.bfloat16),
        ],
        compiler_params=pltpu.CompilerParams(vmem_limit_bytes=24 * 1024 * 1024),
        name="convolve",
    )(cols, taps, jnp.asarray(high), jnp.asarray(low), jnp.asarray(inverse))


def on_device(query, key, value, upstream, taps):
    seq, chan = lax.axis_size("seq"), lax.axis_size("chan")
    wide, positions = query.shape
    chans = wide // seq
    mixed = (key * value).reshape(seq, chans, positions)
    pulled = (upstream * query).reshape(seq, chans, positions)
    sent = jnp.concatenate([mixed, pulled], axis=1)
    cols = lax.all_to_all(sent, "seq", split_axis=0, concat_axis=0)
    out_cols, lag = convolve(cols, taps, chan)
    rows = lax.all_to_all(out_cols, "seq", split_axis=0, concat_axis=0)
    lags = lax.all_to_all(lag, "chan", split_axis=0, concat_axis=0)
    filter_grad = jnp.sum(lags.astype(jnp.float32), axis=0)
    conv = rows[:, :chans].reshape(wide, positions)
    back = rows[:, chans:].reshape(wide, positions)
    return query * conv, upstream * conv, back * value, back * key, filter_grad


def solution(mesh):
    block = P("chan", "seq")
    return jax.shard_map(
        on_device,
        mesh=mesh,
        in_specs=(block, block, block, block, P("seq", None)),
        out_specs=(block, block, block, block, P("seq", "chan")),
        check_vma=False,
    )
```

```python
import functools
import math

import jax
import jax.numpy as jnp
import ml_dtypes
import numpy as np
from jax import lax
from jax.experimental import pallas as pl
from jax.experimental.pallas import tpu as pltpu
from jax.sharding import PartitionSpec as P

BLOCK = 256
LANES = 128


def transform_tables(scale):
    freq = np.arange(BLOCK) + 0.5
    freq = np.concatenate([freq[0::2], freq[1::2]])
    angle = 2.0 * np.pi * np.outer(np.arange(BLOCK), freq) / (2 * BLOCK)
    forward = np.concatenate([np.cos(angle), -np.sin(angle)], axis=1)
    inverse = np.concatenate([np.cos(angle).T, -np.sin(angle).T], axis=0) * (scale / BLOCK)
    high = forward.astype(ml_dtypes.bfloat16)
    low = (forward - high.astype(np.float64)).astype(ml_dtypes.bfloat16)
    return high, low, inverse.astype(ml_dtypes.bfloat16)


def dot(left, right):
    return jnp.dot(left, right, preferred_element_type=jnp.float32)


def total(terms):
    real, imag = terms[0]
    for more_real, more_imag in terms[1:]:
        real, imag = real + more_real, imag + more_imag
    return real, imag


def times(left, right):
    return left[0] * right[0] - left[1] * right[1], left[0] * right[1] + left[1] * right[0]


def times_conj(left, right):
    return left[0] * right[0] + left[1] * right[1], left[1] * right[0] - left[0] * right[1]


def place():
    me = lax.axis_index("seq")
    return me // 2, me % 2


def forward(block, high_ref, low_ref):
    return dot(block, high_ref[...]) + dot(block, low_ref[...])


def tiles(chans, body):
    tile = 16 if chans % 16 == 0 else chans

    def step(i, carry):
        rows = pl.ds(pl.multiple_of(i * tile, tile), tile)
        for half in range(BLOCK // LANES):
            sign = 1.0 if half < BLOCK // LANES // 2 else -1.0
            body(rows, pl.ds(half * LANES, LANES), pl.ds(BLOCK + half * LANES, LANES), sign)
        return carry

    lax.fori_loop(0, chans // tile, step, 0)


def spectra(ref, rows, re, im):
    return [(ref[a, rows, re], ref[a, rows, im]) for a in range(ref.shape[0])]


def convolve_tile(signal, taps, sign, put):
    before = None
    for c in range(len(signal)):
        here = total([times(signal[a], taps[c - a]) for a in range(c + 1)])
        put(c, here if c == 0 else (here[0] - sign * before[1], here[1] + sign * before[0]))
        before = here


def correlate_tile(signal, other, sign, put):
    after = None
    for c in reversed(range(len(signal))):
        here = total([times_conj(signal[a], other[a - c]) for a in range(c, len(signal))])
        put(c, here if after is None else (here[0] + sign * after[1], here[1] - sign * after[0]))
        after = here


def putter(prod, rows, re, im):
    def put(c, value):
        prod[c, rows, re] = value[0].astype(jnp.bfloat16)
        prod[c, rows, im] = value[1].astype(jnp.bfloat16)

    return put


def gate_kernel(*refs):
    sources, held, (own_ref, other_ref, sems) = refs[:4], refs[4:8], refs[8:]
    chip, core = place()
    copies = [pltpu.make_async_copy(a, b, sems.at[i]) for i, (a, b) in enumerate(zip(sources, held))]
    for copy in copies:
        copy.start()
    for i in range(2):
        left, right = held[2 * i], held[2 * i + 1]
        copies[2 * i].wait()
        copies[2 * i + 1].wait()
        for k in range(own_ref.shape[0]):
            mine, theirs = 2 * (chip ^ k) + core, 2 * (chip ^ k) + 1 - core
            own_ref[k, i] = left[mine] * right[mine]
            other_ref[k, i] = left[theirs] * right[theirs]


def taps_kernel(taps_ref, high_ref, low_ref, filt_ref):
    for a in range(filt_ref.shape[0]):
        filt_ref[a] = forward(taps_ref[:, a * BLOCK : (a + 1) * BLOCK], high_ref, low_ref)


def sides_kernel(*refs):
    count = len(refs) - 9
    cols_refs, refs = refs[:count], refs[count:]
    filt_ref, high_ref, low_ref, inv_ref, own_ref, other_ref, mix_ref, pull_ref, prod = refs
    chip, core = place()
    for i, spec_ref in enumerate((mix_ref, pull_ref)):
        for k in range(count):
            block = jnp.concatenate([cols_refs[k][core, i], cols_refs[k][1 - core, i]], axis=1)
            spec_ref[chip ^ k] = forward(block, high_ref, low_ref)

    def body(rows, re, im, sign):
        taps = spectra(filt_ref, rows, re, im)
        convolve_tile(spectra(mix_ref, rows, re, im), taps, sign, putter(prod.at[0], rows, re, im))
        correlate_tile(spectra(pull_ref, rows, re, im), taps, sign, putter(prod.at[1], rows, re, im))

    tiles(filt_ref.shape[1], body)
    for k in range(count):
        for i in range(2):
            result = dot(prod[i, chip ^ k], inv_ref[...]).astype(jnp.bfloat16)
            first, second = result[:, :LANES], result[:, LANES:]
            own_ref[k, i] = jnp.where(core == 0, first, second)
            other_ref[k, i] = jnp.where(core == 0, second, first)


def lag_kernel(pull_ref, mix_ref, inv_ref, lag_ref, prod):
    width = lag_ref.shape[2]
    slot = lax.axis_index("chan")

    def body(rows, re, im, sign):
        correlate_tile(spectra(pull_ref, rows, re, im), spectra(mix_ref, rows, re, im), sign, putter(prod, rows, re, im))

    tiles(prod.shape[1], body)
    for c in range(prod.shape[0]):
        result = dot(prod[c], inv_ref[...]).astype(jnp.bfloat16)
        for u in range(BLOCK // LANES):
            begin = c * BLOCK + u * LANES
            lag_ref[slot ^ (begin // width), :, begin % width : begin % width + LANES] = result[:, u * LANES : (u + 1) * LANES]


def grads_kernel(count, *refs):
    rows_refs, (query_ref, key_ref, value_ref, upstream_ref) = refs[:count], refs[count : count + 4]
    lag_ref, got_refs = refs[count + 4], refs[count + 5 : -9]
    outs, filter_out, (held, sems, sums, sum_sem) = refs[-9:-5], refs[-5], refs[-4:]
    chip, core = place()
    total_lag = lag_ref[0].astype(jnp.float32)
    for got in got_refs:
        total_lag = total_lag + got[...].astype(jnp.float32)
    sums[...] = total_lag
    copies = [pltpu.make_async_copy(sums, filter_out, sum_sem)]
    copies[0].start()
    for k in range(count):
        there = 2 * (chip ^ k)
        for at in range(2):
            group = there + at
            conv, back = rows_refs[k][core ^ at, 0], rows_refs[k][core ^ at, 1]
            held[0, 2 * k + at] = conv * query_ref[group]
            held[1, 2 * k + at] = conv * upstream_ref[group]
            held[2, 2 * k + at] = back * value_ref[group]
            held[3, 2 * k + at] = back * key_ref[group]
        for i, out in enumerate(outs):
            copy = pltpu.make_async_copy(held.at[i, pl.ds(2 * k, 2)], out.at[pl.ds(there, 2)], sems.at[i, k])
            copy.start()
            copies.append(copy)
    for copy in copies:
        copy.wait()


VMEM = pl.BlockSpec(memory_space=pltpu.VMEM)
ANY = pl.BlockSpec(memory_space=pl.ANY)
HBM = pl.BlockSpec(memory_space=pltpu.HBM)
LIMIT = 16 * 1024 * 1024


def call(kernel, args, outs, scratch, name, space=VMEM, out_space=VMEM, after=(), flops=0):
    def body(*refs):
        kernel(*refs[: len(args)], *refs[len(args) + len(after) :])

    return pl.pallas_call(
        body,
        out_shape=tuple(jax.ShapeDtypeStruct(shape, kind) for shape, kind in outs),
        in_specs=[space] * len(args) + [ANY] * len(after),
        out_specs=(out_space,) * len(outs),
        scratch_shapes=scratch,
        compiler_params=pltpu.CompilerParams(vmem_limit_bytes=LIMIT),
        cost_estimate=pl.CostEstimate(flops=flops, bytes_accessed=0, transcendentals=0) if flops else None,
        name=name,
    )(*args, *after)


def swap(array, axis, k):
    return lax.ppermute(array, axis, [(i, i ^ k) for i in range(lax.axis_size(axis))])


def exchange(own, other):
    got = swap(other, "seq", 1)
    parts = [jnp.stack([own[k], got[k]]) for k in range(own.shape[0])]
    return [parts[0]] + [swap(parts[k], "seq", 2 * k) for k in range(1, len(parts))]


def on_device(query, key, value, upstream, taps):
    seq, chan = lax.axis_size("seq"), lax.axis_size("chan")
    wide, positions = query.shape
    chans, length = taps.shape
    count = seq // 2
    query, key, value, upstream = (x.reshape(seq, chans, positions) for x in (query, key, value, upstream))
    high, low, inverse = (jnp.asarray(x) for x in transform_tables(1.0 / math.sqrt(length)))
    half = ((count, 2, chans, positions), jnp.bfloat16)
    whole = ((seq, chans, positions), jnp.bfloat16)
    wave = ((count, chans, 2 * BLOCK), jnp.float32)
    key, value, upstream, query, own, other = call(
        gate_kernel,
        tuple(pltpu.with_memory_space_constraint(x, pltpu.HBM) for x in (key, value, upstream, query)),
        (whole,) * 4 + (half,) * 2,
        [pltpu.SemaphoreType.DMA((4,))],
        "gate",
        HBM,
    )
    cols = exchange(own, other)
    (filt,) = call(taps_kernel, (taps, high, low), (wave,), [], "taps")
    own, other, mix_wave, pull_wave = call(
        sides_kernel,
        (*cols, filt, high, low, inverse),
        (half, half, wave, wave),
        [pltpu.VMEM((2, count, chans, 2 * BLOCK), jnp.bfloat16)],
        "sides",
    )
    rows = exchange(own, other)
    pieces = ((chan, chans, length // chan), jnp.bfloat16)
    prod = pltpu.VMEM((count, chans, 2 * BLOCK), jnp.bfloat16)
    (lag,) = call(lag_kernel, (pull_wave, mix_wave, inverse), (pieces,), [prod], "lag", after=(own,))
    got = [swap(lag[k], "chan", k) for k in range(1, chan)]
    sums = ((chans, length // chan), jnp.float32)
    *outs, filter_grad = call(
        functools.partial(grads_kernel, count),
        (*rows, query, key, value, upstream, lag, *got),
        (whole,) * 4 + (sums,),
        [
            pltpu.VMEM((4, seq, chans, positions), jnp.bfloat16),
            pltpu.SemaphoreType.DMA((4, count)),
            pltpu.VMEM(*sums),
            pltpu.SemaphoreType.DMA,
        ],
        "grads",
        out_space=HBM,
    )
    return (*(x.reshape(wide, positions) for x in outs), filter_grad)


def solution(mesh):
    block = P("chan", "seq")
    return jax.shard_map(
        on_device,
        mesh=mesh,
        in_specs=(block, block, block, block, P("seq", None)),
        out_specs=(block, block, block, block, P("seq", "chan")),
        check_vma=False,
    )
```

```python
import functools
import math

import jax
import jax.numpy as jnp
import ml_dtypes
import numpy as np
from jax import lax
from jax.experimental import pallas as pl
from jax.experimental.pallas import tpu as pltpu
from jax.sharding import PartitionSpec as P

BLOCK = 256
LANES = 128


def transform_tables(scale):
    freq = np.arange(BLOCK) + 0.5
    freq = np.concatenate([freq[0::2], freq[1::2]])
    angle = 2.0 * np.pi * np.outer(np.arange(BLOCK), freq) / (2 * BLOCK)
    forward = np.concatenate([np.cos(angle), -np.sin(angle)], axis=1)
    inverse = np.concatenate([np.cos(angle).T, -np.sin(angle).T], axis=0) * (scale / BLOCK)
    high = forward.astype(ml_dtypes.bfloat16)
    low = (forward - high.astype(np.float64)).astype(ml_dtypes.bfloat16)
    return high, low, inverse.astype(ml_dtypes.bfloat16)


def dot(left, right):
    return jnp.dot(left, right, preferred_element_type=jnp.float32)


def total(terms):
    real, imag = terms[0]
    for more_real, more_imag in terms[1:]:
        real, imag = real + more_real, imag + more_imag
    return real, imag


def times(left, right):
    return left[0] * right[0] - left[1] * right[1], left[0] * right[1] + left[1] * right[0]


def times_conj(left, right):
    return left[0] * right[0] + left[1] * right[1], left[1] * right[0] - left[0] * right[1]


def place():
    me = lax.axis_index("seq")
    return me // 2, me % 2


def forward(block, high_ref, low_ref):
    return dot(block, high_ref[...]) + dot(block, low_ref[...])


def tiles(chans, body):
    tile = 16 if chans % 16 == 0 else chans

    def step(i, carry):
        rows = pl.ds(pl.multiple_of(i * tile, tile), tile)
        for half in range(BLOCK // LANES):
            sign = 1.0 if half < BLOCK // LANES // 2 else -1.0
            body(rows, pl.ds(half * LANES, LANES), pl.ds(BLOCK + half * LANES, LANES), sign)
        return carry

    lax.fori_loop(0, chans // tile, step, 0)


def spectra(ref, rows, re, im):
    return [(ref[a, rows, re], ref[a, rows, im]) for a in range(ref.shape[0])]


def convolve_tile(signal, taps, sign, put):
    before = None
    for c in range(len(signal)):
        here = total([times(signal[a], taps[c - a]) for a in range(c + 1)])
        put(c, here if c == 0 else (here[0] - sign * before[1], here[1] + sign * before[0]))
        before = here


def correlate_tile(signal, other, sign, put):
    after = None
    for c in reversed(range(len(signal))):
        here = total([times_conj(signal[a], other[a - c]) for a in range(c, len(signal))])
        put(c, here if after is None else (here[0] + sign * after[1], here[1] - sign * after[0]))
        after = here


def putter(prod, rows, re, im):
    def put(c, value):
        prod[c, rows, re] = value[0].astype(jnp.bfloat16)
        prod[c, rows, im] = value[1].astype(jnp.bfloat16)

    return put


def gate_kernel(*refs):
    sources, held, (own_ref, other_ref, sems) = refs[:4], refs[4:8], refs[8:]
    chip, core = place()
    copies = [pltpu.make_async_copy(a, b, sems.at[i]) for i, (a, b) in enumerate(zip(sources, held))]
    for copy in copies:
        copy.start()
    for i in range(2):
        left, right = held[2 * i], held[2 * i + 1]
        copies[2 * i].wait()
        copies[2 * i + 1].wait()
        for k in range(own_ref.shape[0]):
            mine, theirs = 2 * (chip ^ k) + core, 2 * (chip ^ k) + 1 - core
            own_ref[k, i] = left[mine] * right[mine]
            other_ref[k, i] = left[theirs] * right[theirs]


def taps_kernel(taps_ref, high_ref, low_ref, filt_ref):
    for a in range(filt_ref.shape[0]):
        filt_ref[a] = forward(taps_ref[:, a * BLOCK : (a + 1) * BLOCK], high_ref, low_ref)


def sides_kernel(*refs):
    count = len(refs) - 9
    cols_refs, refs = refs[:count][::-1], refs[count:]
    filt_ref, high_ref, low_ref, inv_ref, own_ref, other_ref, mix_ref, pull_ref, prod = refs
    chip, core = place()
    for i, spec_ref in enumerate((mix_ref, pull_ref)):
        for k in range(count):
            block = jnp.concatenate([cols_refs[k][core, i], cols_refs[k][1 - core, i]], axis=1)
            spec_ref[chip ^ k] = forward(block, high_ref, low_ref)

    def body(rows, re, im, sign):
        taps = spectra(filt_ref, rows, re, im)
        convolve_tile(spectra(mix_ref, rows, re, im), taps, sign, putter(prod.at[0], rows, re, im))
        correlate_tile(spectra(pull_ref, rows, re, im), taps, sign, putter(prod.at[1], rows, re, im))

    tiles(filt_ref.shape[1], body)
    for k in range(count):
        for i in range(2):
            result = dot(prod[i, chip ^ k], inv_ref[...]).astype(jnp.bfloat16)
            first, second = result[:, :LANES], result[:, LANES:]
            own_ref[k, i] = jnp.where(core == 0, first, second)
            other_ref[k, i] = jnp.where(core == 0, second, first)


def reversed_bits(number, size):
    bits = size.bit_length() - 1
    return sum((number // 2**i % 2) * 2 ** (bits - 1 - i) for i in range(bits))


def lag_kernel(pull_ref, mix_ref, inv_ref, lag_ref, prod):
    width = lag_ref.shape[2]
    slot = lax.axis_index("chan")

    def body(rows, re, im, sign):
        correlate_tile(spectra(pull_ref, rows, re, im), spectra(mix_ref, rows, re, im), sign, putter(prod, rows, re, im))

    tiles(prod.shape[1], body)
    for c in range(prod.shape[0]):
        result = dot(prod[c], inv_ref[...]).astype(jnp.bfloat16)
        for u in range(BLOCK // LANES):
            begin = c * BLOCK + u * LANES
            at = reversed_bits(slot ^ (begin // width), lag_ref.shape[0])
            lag_ref[at, :, begin % width : begin % width + LANES] = result[:, u * LANES : (u + 1) * LANES]


def grads_kernel(count, *refs):
    rows_refs, (query_ref, key_ref, value_ref, upstream_ref) = refs[:count][::-1], refs[count : count + 4]
    kept_ref, got_ref = refs[count + 4 : count + 6]
    outs, filter_out, (held, sems, sums, sum_sem) = refs[-9:-5], refs[-5], refs[-4:]
    chip, core = place()
    sums[...] = kept_ref[0].astype(jnp.float32) + got_ref[0].astype(jnp.float32)
    copies = [pltpu.make_async_copy(sums, filter_out, sum_sem)]
    copies[0].start()
    for k in range(count):
        there = 2 * (chip ^ k)
        for at in range(2):
            group = there + at
            conv, back = rows_refs[k][core ^ at, 0], rows_refs[k][core ^ at, 1]
            held[0, 2 * k + at] = conv * query_ref[group]
            held[1, 2 * k + at] = conv * upstream_ref[group]
            held[2, 2 * k + at] = back * value_ref[group]
            held[3, 2 * k + at] = back * key_ref[group]
        for i, out in enumerate(outs):
            copy = pltpu.make_async_copy(held.at[i, pl.ds(2 * k, 2)], out.at[pl.ds(there, 2)], sems.at[i, k])
            copy.start()
            copies.append(copy)
    for copy in copies:
        copy.wait()


VMEM = pl.BlockSpec(memory_space=pltpu.VMEM)
ANY = pl.BlockSpec(memory_space=pl.ANY)
HBM = pl.BlockSpec(memory_space=pltpu.HBM)
LIMIT = 16 * 1024 * 1024


def call(kernel, args, outs, scratch, name, space=VMEM, out_space=VMEM, after=(), flops=0):
    def body(*refs):
        kernel(*refs[: len(args)], *refs[len(args) + len(after) :])

    return pl.pallas_call(
        body,
        out_shape=tuple(jax.ShapeDtypeStruct(shape, kind) for shape, kind in outs),
        in_specs=[space] * len(args) + [ANY] * len(after),
        out_specs=(out_space,) * len(outs),
        scratch_shapes=scratch,
        compiler_params=pltpu.CompilerParams(vmem_limit_bytes=LIMIT),
        cost_estimate=pl.CostEstimate(flops=flops, bytes_accessed=0, transcendentals=0) if flops else None,
        name=name,
    )(*args, *after)


def swap(array, axis, k):
    return lax.ppermute(array, axis, [(i, i ^ k) for i in range(lax.axis_size(axis))])


def exchange(own, other):
    got = swap(other, "seq", 1)
    parts = [jnp.stack([own[k], got[k]]) for k in range(own.shape[0])]
    moved = [swap(parts[k], "seq", 2 * k) for k in reversed(range(1, len(parts)))]
    return moved + [parts[0]], got


def scatter_sum(pieces):
    size, step = pieces.shape[0], 1
    while True:
        kept, sent = pieces[: size // 2], pieces[size // 2 :].astype(jnp.bfloat16)
        got = swap(sent, "chan", step)
        if size == 2:
            return kept, got
        pieces = kept.astype(jnp.float32) + got.astype(jnp.float32)
        size, step = size // 2, step * 2


def on_device(query, key, value, upstream, taps):
    seq, chan = lax.axis_size("seq"), lax.axis_size("chan")
    wide, positions = query.shape
    chans, length = taps.shape
    count = seq // 2
    query, key, value, upstream = (x.reshape(seq, chans, positions) for x in (query, key, value, upstream))
    high, low, inverse = (jnp.asarray(x) for x in transform_tables(1.0 / math.sqrt(length)))
    half = ((count, 2, chans, positions), jnp.bfloat16)
    whole = ((seq, chans, positions), jnp.bfloat16)
    wave = ((count, chans, 2 * BLOCK), jnp.float32)
    key, value, upstream, query, own, other = call(
        gate_kernel,
        tuple(pltpu.with_memory_space_constraint(x, pltpu.HBM) for x in (key, value, upstream, query)),
        (whole,) * 4 + (half,) * 2,
        [pltpu.SemaphoreType.DMA((4,))],
        "gate",
        HBM,
    )
    cols, _ = exchange(own, other)
    (filt,) = call(taps_kernel, (taps, high, low), (wave,), [], "taps")
    own, other, mix_wave, pull_wave = call(
        sides_kernel,
        (*cols, filt, high, low, inverse),
        (half, half, wave, wave),
        [pltpu.VMEM((2, count, chans, 2 * BLOCK), jnp.bfloat16)],
        "sides",
    )
    rows, swapped = exchange(own, other)
    pieces = ((chan, chans, length // chan), jnp.bfloat16)
    prod = pltpu.VMEM((count, chans, 2 * BLOCK), jnp.bfloat16)
    (lag,) = call(lag_kernel, (pull_wave, mix_wave, inverse), (pieces,), [prod], "lag", after=(own,))
    lag, _ = lax.optimization_barrier((lag, swapped))
    kept, got = scatter_sum(lag)
    sums = ((chans, length // chan), jnp.float32)
    *outs, filter_grad = call(
        functools.partial(grads_kernel, count),
        (*rows, query, key, value, upstream, kept, got),
        (whole,) * 4 + (sums,),
        [
            pltpu.VMEM((4, seq, chans, positions), jnp.bfloat16),
            pltpu.SemaphoreType.DMA((4, count)),
            pltpu.VMEM(*sums),
            pltpu.SemaphoreType.DMA,
        ],
        "grads",
        out_space=HBM,
    )
    return (*(x.reshape(wide, positions) for x in outs), filter_grad)


def solution(mesh):
    block = P("chan", "seq")
    return jax.shard_map(
        on_device,
        mesh=mesh,
        in_specs=(block, block, block, block, P("seq", None)),
        out_specs=(block, block, block, block, P("seq", "chan")),
        check_vma=False,
    )
```

```python
import functools
import math

import jax
import jax.numpy as jnp
import ml_dtypes
import numpy as np
from jax import lax
from jax.experimental import pallas as pl
from jax.experimental.pallas import tpu as pltpu
from jax.sharding import PartitionSpec as P

BLOCK = 256
LANES = 128


def transform_tables(scale):
    freq = np.arange(BLOCK) + 0.5
    freq = np.concatenate([freq[0::2], freq[1::2]])
    angle = 2.0 * np.pi * np.outer(np.arange(BLOCK), freq) / (2 * BLOCK)
    forward = np.concatenate([np.cos(angle), -np.sin(angle)], axis=1)
    inverse = np.concatenate([np.cos(angle).T, -np.sin(angle).T], axis=0) * (scale / BLOCK)
    high = forward.astype(ml_dtypes.bfloat16)
    low = (forward - high.astype(np.float64)).astype(ml_dtypes.bfloat16)
    return high, low, inverse.astype(ml_dtypes.bfloat16)


def dot(left, right):
    return jnp.dot(left, right, preferred_element_type=jnp.float32)


def total(terms):
    real, imag = terms[0]
    for more_real, more_imag in terms[1:]:
        real, imag = real + more_real, imag + more_imag
    return real, imag


def times(left, right):
    return left[0] * right[0] - left[1] * right[1], left[0] * right[1] + left[1] * right[0]


def times_conj(left, right):
    return left[0] * right[0] + left[1] * right[1], left[1] * right[0] - left[0] * right[1]


def place():
    me = lax.axis_index("seq")
    return me // 2, me % 2


def forward(block, high_ref, low_ref):
    return dot(block, high_ref[...]) + dot(block, low_ref[...])


def tiles(chans, body):
    tile = 16 if chans % 16 == 0 else chans

    def step(i, carry):
        rows = pl.ds(pl.multiple_of(i * tile, tile), tile)
        for half in range(BLOCK // LANES):
            sign = 1.0 if half < BLOCK // LANES // 2 else -1.0
            body(rows, pl.ds(half * LANES, LANES), pl.ds(BLOCK + half * LANES, LANES), sign)
        return carry

    lax.fori_loop(0, chans // tile, step, 0, unroll=True)


def spectra(ref, rows, re, im):
    return [(ref[a, rows, re], ref[a, rows, im]) for a in range(ref.shape[0])]


def convolve_tile(signal, taps, sign, put):
    before = None
    for c in range(len(signal)):
        here = total([times(signal[a], taps[c - a]) for a in range(c + 1)])
        put(c, here if c == 0 else (here[0] - sign * before[1], here[1] + sign * before[0]))
        before = here


def correlate_tile(signal, other, sign, put):
    after = None
    for c in reversed(range(len(signal))):
        here = total([times_conj(signal[a], other[a - c]) for a in range(c, len(signal))])
        put(c, here if after is None else (here[0] + sign * after[1], here[1] - sign * after[0]))
        after = here


def putter(prod, rows, re, im):
    def put(c, value):
        prod[c, rows, re] = value[0].astype(jnp.bfloat16)
        prod[c, rows, im] = value[1].astype(jnp.bfloat16)

    return put


def gate_kernel(*refs):
    sources, held, (own_ref, other_ref, sems) = refs[:4], refs[4:8], refs[8:]
    chip, core = place()
    copies = [pltpu.make_async_copy(a, b, sems.at[i]) for i, (a, b) in enumerate(zip(sources, held))]
    for copy in copies:
        copy.start()
    for i in range(2):
        left, right = held[2 * i], held[2 * i + 1]
        copies[2 * i].wait()
        copies[2 * i + 1].wait()
        for k in range(own_ref.shape[0]):
            mine, theirs = 2 * (chip ^ k) + core, 2 * (chip ^ k) + 1 - core
            own_ref[k, i] = left[mine] * right[mine]
            other_ref[k, i] = left[theirs] * right[theirs]


def taps_kernel(taps_ref, high_ref, low_ref, filt_ref):
    for a in range(filt_ref.shape[0]):
        filt_ref[a] = forward(taps_ref[:, a * BLOCK : (a + 1) * BLOCK], high_ref, low_ref)


def far(k):
    return k.bit_count() > 1


def early(count):
    return [k for k in range(count) if k == 0 or far(k)]


def late(count):
    return [k for k in range(count) if k and not far(k)]


def early_pieces(refs, count):
    size = len(early(count))
    pieces = [(refs[2 * i], refs[2 * i + 1]) for i in range(size)]
    pieces[0] = pieces[0][0].at[0], pieces[0][1].at[0]
    return list(zip(early(count), pieces)), refs[2 * size :]


def late_pieces(refs, count):
    size = len(late(count))
    return [(k, (refs[i].at[0], refs[i].at[1])) for i, k in enumerate(late(count))], refs[size:]


def transform(pair, i, high_ref, low_ref):
    chip, core = place()
    mine, theirs = pair[0][i], pair[1][i]
    halves = [jnp.where(core == 0, mine, theirs), jnp.where(core == 0, theirs, mine)]
    return forward(jnp.concatenate(halves, axis=1), high_ref, low_ref)


def early_kernel(count, *refs):
    pieces, (high_ref, low_ref, wave_ref) = early_pieces(refs, count)
    for at, (k, pair) in enumerate(pieces):
        for i in range(2):
            wave_ref[at, i] = transform(pair, i, high_ref, low_ref)


def sides_kernel(count, *refs):
    pieces, refs = late_pieces(refs, count)
    wave_ref, filt_ref, high_ref, low_ref, inv_ref, own_ref, other_ref, mix_ref, pull_ref, prod = refs
    chip, core = place()
    for i, spec_ref in enumerate((mix_ref, pull_ref)):
        for at, k in enumerate(early(count)):
            spec_ref[chip ^ k] = wave_ref[at, i]
        for k, pair in pieces:
            spec_ref[chip ^ k] = transform(pair, i, high_ref, low_ref)

    def body(rows, re, im, sign):
        taps = spectra(filt_ref, rows, re, im)
        convolve_tile(spectra(mix_ref, rows, re, im), taps, sign, putter(prod.at[0], rows, re, im))
        correlate_tile(spectra(pull_ref, rows, re, im), taps, sign, putter(prod.at[1], rows, re, im))

    tiles(filt_ref.shape[1], body)
    for k in range(count):
        for i in range(2):
            result = dot(prod[i, chip ^ k], inv_ref[...]).astype(jnp.bfloat16)
            first, second = result[:, :LANES], result[:, LANES:]
            own_ref[k, i] = jnp.where(core == 0, first, second)
            other_ref[k, i] = jnp.where(core == 0, second, first)


def reversed_bits(number, size):
    bits = size.bit_length() - 1
    return sum((number // 2**i % 2) * 2 ** (bits - 1 - i) for i in range(bits))


def lag_kernel(pull_ref, mix_ref, inv_ref, lag_ref, prod):
    width = lag_ref.shape[2]
    slot = lax.axis_index("chan")

    def body(rows, re, im, sign):
        correlate_tile(spectra(pull_ref, rows, re, im), spectra(mix_ref, rows, re, im), sign, putter(prod, rows, re, im))

    tiles(prod.shape[1], body)
    for c in range(prod.shape[0]):
        result = dot(prod[c], inv_ref[...]).astype(jnp.bfloat16)
        for u in range(BLOCK // LANES):
            begin = c * BLOCK + u * LANES
            at = reversed_bits(slot ^ (begin // width), lag_ref.shape[0])
            lag_ref[at, :, begin % width : begin % width + LANES] = result[:, u * LANES : (u + 1) * LANES]


def grads_kernel(count, *refs):
    rows_refs, (query_ref, key_ref, value_ref, upstream_ref) = refs[:count][::-1], refs[count : count + 4]
    kept_ref, got_ref = refs[count + 4 : count + 6]
    outs, filter_out, (held, sems, sums, sum_sem) = refs[-9:-5], refs[-5], refs[-4:]
    chip, core = place()
    sums[...] = kept_ref[0].astype(jnp.float32) + got_ref[0].astype(jnp.float32)
    copies = [pltpu.make_async_copy(sums, filter_out, sum_sem)]
    copies[0].start()
    for k in range(count):
        there = 2 * (chip ^ k)
        for at in range(2):
            group = there + at
            conv, back = rows_refs[k][core ^ at, 0], rows_refs[k][core ^ at, 1]
            held[0, 2 * k + at] = conv * query_ref[group]
            held[1, 2 * k + at] = conv * upstream_ref[group]
            held[2, 2 * k + at] = back * value_ref[group]
            held[3, 2 * k + at] = back * key_ref[group]
        for i, out in enumerate(outs):
            copy = pltpu.make_async_copy(held.at[i, pl.ds(2 * k, 2)], out.at[pl.ds(there, 2)], sems.at[i, k])
            copy.start()
            copies.append(copy)
    for copy in copies:
        copy.wait()


VMEM = pl.BlockSpec(memory_space=pltpu.VMEM)
ANY = pl.BlockSpec(memory_space=pl.ANY)
HBM = pl.BlockSpec(memory_space=pltpu.HBM)
LIMIT = 16 * 1024 * 1024


def call(kernel, args, outs, scratch, name, space=VMEM, out_space=VMEM, after=(), flops=0):
    def body(*refs):
        kernel(*refs[: len(args)], *refs[len(args) + len(after) :])

    return pl.pallas_call(
        body,
        out_shape=tuple(jax.ShapeDtypeStruct(shape, kind) for shape, kind in outs),
        in_specs=[space] * len(args) + [ANY] * len(after),
        out_specs=(out_space,) * len(outs),
        scratch_shapes=scratch,
        compiler_params=pltpu.CompilerParams(vmem_limit_bytes=LIMIT),
        cost_estimate=pl.CostEstimate(flops=flops, bytes_accessed=0, transcendentals=0) if flops else None,
        name=name,
    )(*args, *after)


def swap(array, axis, k):
    return lax.ppermute(array, axis, [(i, i ^ k) for i in range(lax.axis_size(axis))])


def exchange(own, other, split):
    count = own.shape[0]
    got = swap(other, "seq", 1)
    if not split:
        parts = [jnp.stack([own[k], got[k]]) for k in range(count)]
        return [*(swap(parts[k], "seq", 2 * k) for k in reversed(range(1, count))), parts[0]], got
    first = [own, got]
    for k in early(count)[1:]:
        first += [swap(own[k], "seq", 2 * k), swap(got[k], "seq", 2 * k)]
    return first, [swap(jnp.stack([own[k], got[k]]), "seq", 2 * k) for k in late(count)]


def scatter_sum(pieces):
    size, step = pieces.shape[0], 1
    while True:
        kept, sent = pieces[: size // 2], pieces[size // 2 :].astype(jnp.bfloat16)
        got = swap(sent, "chan", step)
        if size == 2:
            return kept, got
        pieces = kept.astype(jnp.float32) + got.astype(jnp.float32)
        size, step = size // 2, step * 2


def on_device(query, key, value, upstream, taps):
    seq, chan = lax.axis_size("seq"), lax.axis_size("chan")
    wide, positions = query.shape
    chans, length = taps.shape
    count = seq // 2
    query, key, value, upstream = (x.reshape(seq, chans, positions) for x in (query, key, value, upstream))
    high, low, inverse = (jnp.asarray(x) for x in transform_tables(1.0 / math.sqrt(length)))
    half = ((count, 2, chans, positions), jnp.bfloat16)
    whole = ((seq, chans, positions), jnp.bfloat16)
    wave = ((count, chans, 2 * BLOCK), jnp.float32)
    key, value, upstream, query, own, other = call(
        gate_kernel,
        tuple(pltpu.with_memory_space_constraint(x, pltpu.HBM) for x in (key, value, upstream, query)),
        (whole,) * 4 + (half,) * 2,
        [pltpu.SemaphoreType.DMA((4,))],
        "gate",
        HBM,
    )
    first, rest = exchange(own, other, True)
    (filt,) = call(taps_kernel, (taps, high, low), (wave,), [], "taps")
    waves = ((len(early(count)), 2, chans, 2 * BLOCK), jnp.float32)
    (begun,) = call(functools.partial(early_kernel, count), (*first, high, low), (waves,), [], "early", flops=int(2e+09))
    own, other, mix_wave, pull_wave = call(
        functools.partial(sides_kernel, count),
        (*rest, begun, filt, high, low, inverse),
        (half, half, wave, wave),
        [pltpu.VMEM((2, count, chans, 2 * BLOCK), jnp.bfloat16)],
        "sides",
    )
    rows, swapped = exchange(own, other, False)
    pieces = ((chan, chans, length // chan), jnp.bfloat16)
    prod = pltpu.VMEM((count, chans, 2 * BLOCK), jnp.bfloat16)
    (lag,) = call(lag_kernel, (pull_wave, mix_wave, inverse), (pieces,), [prod], "lag", after=(own,))
    lag, _ = lax.optimization_barrier((lag, swapped))
    kept, got = scatter_sum(lag)
    sums = ((chans, length // chan), jnp.float32)
    *outs, filter_grad = call(
        functools.partial(grads_kernel, count),
        (*rows, query, key, value, upstream, kept, got),
        (whole,) * 4 + (sums,),
        [
            pltpu.VMEM((4, seq, chans, positions), jnp.bfloat16),
            pltpu.SemaphoreType.DMA((4, count)),
            pltpu.VMEM(*sums),
            pltpu.SemaphoreType.DMA,
        ],
        "grads",
        out_space=HBM,
    )
    return (*(x.reshape(wide, positions) for x in outs), filter_grad)


def solution(mesh):
    block = P("chan", "seq")
    return jax.shard_map(
        on_device,
        mesh=mesh,
        in_specs=(block, block, block, block, P("seq", None)),
        out_specs=(block, block, block, block, P("seq", "chan")),
        check_vma=False,
    )
```

```python
import functools
import math

import jax
import jax.numpy as jnp
import ml_dtypes
import numpy as np
from jax import lax
from jax.experimental import pallas as pl
from jax.experimental.pallas import tpu as pltpu
from jax.sharding import PartitionSpec as P

BLOCK = 256
LANES = 128


def transform_tables(scale):
    freq = np.arange(BLOCK) + 0.5
    freq = np.concatenate([freq[0::2], freq[1::2]])
    angle = 2.0 * np.pi * np.outer(np.arange(BLOCK), freq) / (2 * BLOCK)
    forward = np.concatenate([np.cos(angle), -np.sin(angle)], axis=1)
    inverse = np.concatenate([np.cos(angle).T, -np.sin(angle).T], axis=0) * (scale / BLOCK)
    high = forward.astype(ml_dtypes.bfloat16)
    low = (forward - high.astype(np.float64)).astype(ml_dtypes.bfloat16)
    return high, low, inverse.astype(ml_dtypes.bfloat16)


def dot(left, right):
    return jnp.dot(left, right, preferred_element_type=jnp.float32)


def total(terms):
    real, imag = terms[0]
    for more_real, more_imag in terms[1:]:
        real, imag = real + more_real, imag + more_imag
    return real, imag


def times(left, right):
    return left[0] * right[0] - left[1] * right[1], left[0] * right[1] + left[1] * right[0]


def times_conj(left, right):
    return left[0] * right[0] + left[1] * right[1], left[1] * right[0] - left[0] * right[1]


def place():
    me = lax.axis_index("seq")
    return me // 2, me % 2


def forward(block, high_ref, low_ref):
    return dot(block, high_ref[...]) + dot(block, low_ref[...])


def tiles(chans, body):
    tile = 16 if chans % 16 == 0 else chans

    def step(i, carry):
        rows = pl.ds(pl.multiple_of(i * tile, tile), tile)
        for half in range(BLOCK // LANES):
            sign = 1.0 if half < BLOCK // LANES // 2 else -1.0
            body(rows, pl.ds(half * LANES, LANES), pl.ds(BLOCK + half * LANES, LANES), sign)
        return carry

    lax.fori_loop(0, chans // tile, step, 0, unroll=True)


def spectra(ref, rows, re, im):
    return [(ref[a, rows, re], ref[a, rows, im]) for a in range(ref.shape[0])]


def convolve_tile(signal, taps, sign, put):
    before = None
    for c in range(len(signal)):
        here = total([times(signal[a], taps[c - a]) for a in range(c + 1)])
        put(c, here if c == 0 else (here[0] - sign * before[1], here[1] + sign * before[0]))
        before = here


def correlate_tile(signal, other, sign, put):
    after = None
    for c in reversed(range(len(signal))):
        here = total([times_conj(signal[a], other[a - c]) for a in range(c, len(signal))])
        put(c, here if after is None else (here[0] + sign * after[1], here[1] - sign * after[0]))
        after = here


def putter(prod, rows, re, im):
    def put(c, value):
        prod[c, rows, re] = value[0].astype(jnp.bfloat16)
        prod[c, rows, im] = value[1].astype(jnp.bfloat16)

    return put


def gate_kernel(*refs):
    sources, held, (own_ref, other_ref, sems) = refs[:4], refs[4:8], refs[8:]
    chip, core = place()
    copies = [pltpu.make_async_copy(a, b, sems.at[i]) for i, (a, b) in enumerate(zip(sources, held))]
    for copy in copies:
        copy.start()
    for i in range(2):
        left, right = held[2 * i], held[2 * i + 1]
        copies[2 * i].wait()
        copies[2 * i + 1].wait()
        for k in range(own_ref.shape[0]):
            mine, theirs = 2 * (chip ^ k) + core, 2 * (chip ^ k) + 1 - core
            own_ref[k, i] = left[mine] * right[mine]
            other_ref[k, i] = left[theirs] * right[theirs]


def far(k):
    return k.bit_count() > 1


def early(count):
    return [k for k in range(count) if k == 0 or far(k)]


def late(count):
    return [k for k in range(count) if k and not far(k)]


def early_pieces(refs, count):
    size = len(early(count))
    pieces = [(refs[2 * i], refs[2 * i + 1]) for i in range(size)]
    pieces[0] = pieces[0][0].at[0], pieces[0][1].at[0]
    return list(zip(early(count), pieces)), refs[2 * size :]


def late_pieces(refs, count):
    size = len(late(count))
    return [(k, (refs[i].at[0], refs[i].at[1])) for i, k in enumerate(late(count))], refs[size:]


def transform(pair, i, high_ref, low_ref):
    chip, core = place()
    mine, theirs = pair[0][i], pair[1][i]
    halves = [jnp.where(core == 0, mine, theirs), jnp.where(core == 0, theirs, mine)]
    return forward(jnp.concatenate(halves, axis=1), high_ref, low_ref)


def early_kernel(count, *refs):
    pieces, (taps_ref, high_ref, low_ref, wave_ref, filt_ref) = early_pieces(refs, count)
    for a in range(count):
        filt_ref[a] = forward(taps_ref[:, a * BLOCK : (a + 1) * BLOCK], high_ref, low_ref)
    for at, (k, pair) in enumerate(pieces):
        for i in range(2):
            wave_ref[at, i] = transform(pair, i, high_ref, low_ref)


def sides_kernel(count, *refs):
    pieces, refs = late_pieces(refs, count)
    wave_ref, filt_ref, high_ref, low_ref, inv_ref, own_ref, other_ref, mix_ref, pull_ref, prod = refs
    chip, core = place()
    for i, spec_ref in enumerate((mix_ref, pull_ref)):
        for at, k in enumerate(early(count)):
            spec_ref[chip ^ k] = wave_ref[at, i]
        for k, pair in pieces:
            spec_ref[chip ^ k] = transform(pair, i, high_ref, low_ref)

    def body(rows, re, im, sign):
        taps = spectra(filt_ref, rows, re, im)
        convolve_tile(spectra(mix_ref, rows, re, im), taps, sign, putter(prod.at[0], rows, re, im))
        correlate_tile(spectra(pull_ref, rows, re, im), taps, sign, putter(prod.at[1], rows, re, im))

    tiles(filt_ref.shape[1], body)
    for k in range(count):
        for i in range(2):
            result = dot(prod[i, chip ^ k], inv_ref[...]).astype(jnp.bfloat16)
            first, second = result[:, :LANES], result[:, LANES:]
            own_ref[k, i] = jnp.where(core == 0, first, second)
            other_ref[k, i] = jnp.where(core == 0, second, first)


def reversed_bits(number, size):
    bits = size.bit_length() - 1
    return sum((number // 2**i % 2) * 2 ** (bits - 1 - i) for i in range(bits))


def lag_kernel(pull_ref, mix_ref, inv_ref, lag_ref, prod):
    width = lag_ref.shape[2]
    slot = lax.axis_index("chan")

    def body(rows, re, im, sign):
        correlate_tile(spectra(pull_ref, rows, re, im), spectra(mix_ref, rows, re, im), sign, putter(prod, rows, re, im))

    tiles(prod.shape[1], body)
    for c in range(prod.shape[0]):
        result = dot(prod[c], inv_ref[...]).astype(jnp.bfloat16)
        for u in range(BLOCK // LANES):
            begin = c * BLOCK + u * LANES
            at = reversed_bits(slot ^ (begin // width), lag_ref.shape[0])
            lag_ref[at, :, begin % width : begin % width + LANES] = result[:, u * LANES : (u + 1) * LANES]


def grads_kernel(count, *refs):
    rows_refs, (query_ref, key_ref, value_ref, upstream_ref) = refs[:count][::-1], refs[count : count + 4]
    kept_ref, got_ref = refs[count + 4 : count + 6]
    outs, filter_out, (held, sems, sums, sum_sem) = refs[-9:-5], refs[-5], refs[-4:]
    chip, core = place()
    sums[...] = kept_ref[0].astype(jnp.float32) + got_ref[0].astype(jnp.float32)
    copies = [pltpu.make_async_copy(sums, filter_out, sum_sem)]
    copies[0].start()
    for k in range(count):
        there = 2 * (chip ^ k)
        for at in range(2):
            group = there + at
            conv, back = rows_refs[k][core ^ at, 0], rows_refs[k][core ^ at, 1]
            held[0, 2 * k + at] = conv * query_ref[group]
            held[1, 2 * k + at] = conv * upstream_ref[group]
            held[2, 2 * k + at] = back * value_ref[group]
            held[3, 2 * k + at] = back * key_ref[group]
        for i, out in enumerate(outs):
            copy = pltpu.make_async_copy(held.at[i, pl.ds(2 * k, 2)], out.at[pl.ds(there, 2)], sems.at[i, k])
            copy.start()
            copies.append(copy)
    for copy in copies:
        copy.wait()


VMEM = pl.BlockSpec(memory_space=pltpu.VMEM)
ANY = pl.BlockSpec(memory_space=pl.ANY)
HBM = pl.BlockSpec(memory_space=pltpu.HBM)
LIMIT = 16 * 1024 * 1024


def call(kernel, args, outs, scratch, name, space=VMEM, out_space=VMEM, after=(), flops=0):
    def body(*refs):
        kernel(*refs[: len(args)], *refs[len(args) + len(after) :])

    return pl.pallas_call(
        body,
        out_shape=tuple(jax.ShapeDtypeStruct(shape, kind) for shape, kind in outs),
        in_specs=[space] * len(args) + [ANY] * len(after),
        out_specs=(out_space,) * len(outs),
        scratch_shapes=scratch,
        compiler_params=pltpu.CompilerParams(vmem_limit_bytes=LIMIT),
        cost_estimate=pl.CostEstimate(flops=flops, bytes_accessed=0, transcendentals=0) if flops else None,
        name=name,
    )(*args, *after)


def swap(array, axis, k):
    return lax.ppermute(array, axis, [(i, i ^ k) for i in range(lax.axis_size(axis))])


def exchange(own, other, split):
    count = own.shape[0]
    got = swap(other, "seq", 1)
    if not split:
        parts = [jnp.stack([own[k], got[k]]) for k in range(count)]
        return [*(swap(parts[k], "seq", 2 * k) for k in reversed(range(1, count))), parts[0]], got
    first = [own, got]
    for k in early(count)[1:]:
        first += [swap(own[k], "seq", 2 * k), swap(got[k], "seq", 2 * k)]
    return first, [swap(jnp.stack([own[k], got[k]]), "seq", 2 * k) for k in late(count)]


def scatter_sum(pieces):
    size, step = pieces.shape[0], 1
    while True:
        kept, sent = pieces[: size // 2], pieces[size // 2 :].astype(jnp.bfloat16)
        got = swap(sent, "chan", step)
        if size == 2:
            return kept, got
        pieces = kept.astype(jnp.float32) + got.astype(jnp.float32)
        size, step = size // 2, step * 2


def on_device(query, key, value, upstream, taps):
    seq, chan = lax.axis_size("seq"), lax.axis_size("chan")
    wide, positions = query.shape
    chans, length = taps.shape
    count = seq // 2
    query, key, value, upstream = (x.reshape(seq, chans, positions) for x in (query, key, value, upstream))
    high, low, inverse = (jnp.asarray(x) for x in transform_tables(1.0 / math.sqrt(length)))
    half = ((count, 2, chans, positions), jnp.bfloat16)
    whole = ((seq, chans, positions), jnp.bfloat16)
    wave = ((count, chans, 2 * BLOCK), jnp.float32)
    key, value, upstream, query, own, other = call(
        gate_kernel,
        tuple(pltpu.with_memory_space_constraint(x, pltpu.HBM) for x in (key, value, upstream, query)),
        (whole,) * 4 + (half,) * 2,
        [pltpu.SemaphoreType.DMA((4,))],
        "gate",
        HBM,
    )
    first, rest = exchange(own, other, True)
    waves = ((len(early(count)), 2, chans, 2 * BLOCK), jnp.float32)
    begun, filt = call(functools.partial(early_kernel, count), (*first, taps, high, low), (waves, wave), [], "early", flops=int(2e+09))
    own, other, mix_wave, pull_wave = call(
        functools.partial(sides_kernel, count),
        (*rest, begun, filt, high, low, inverse),
        (half, half, wave, wave),
        [pltpu.VMEM((2, count, chans, 2 * BLOCK), jnp.bfloat16)],
        "sides",
    )
    rows, swapped = exchange(own, other, False)
    pieces = ((chan, chans, length // chan), jnp.bfloat16)
    prod = pltpu.VMEM((count, chans, 2 * BLOCK), jnp.bfloat16)
    (lag,) = call(lag_kernel, (pull_wave, mix_wave, inverse), (pieces,), [prod], "lag", after=(own,))
    lag, _ = lax.optimization_barrier((lag, swapped))
    kept, got = scatter_sum(lag)
    sums = ((chans, length // chan), jnp.float32)
    *outs, filter_grad = call(
        functools.partial(grads_kernel, count),
        (*rows, query, key, value, upstream, kept, got),
        (whole,) * 4 + (sums,),
        [
            pltpu.VMEM((4, seq, chans, positions), jnp.bfloat16),
            pltpu.SemaphoreType.DMA((4, count)),
            pltpu.VMEM(*sums),
            pltpu.SemaphoreType.DMA,
        ],
        "grads",
        out_space=HBM,
    )
    return (*(x.reshape(wide, positions) for x in outs), filter_grad)


def solution(mesh):
    block = P("chan", "seq")
    return jax.shard_map(
        on_device,
        mesh=mesh,
        in_specs=(block, block, block, block, P("seq", None)),
        out_specs=(block, block, block, block, P("seq", "chan")),
        check_vma=False,
    )
```

```python
import functools
import math

import jax
import jax.numpy as jnp
import ml_dtypes
import numpy as np
from jax import lax
from jax.experimental import pallas as pl
from jax.experimental.pallas import tpu as pltpu
from jax.sharding import PartitionSpec as P

BLOCK = 256
LANES = 128


def transform_tables(scale):
    freq = np.arange(BLOCK) + 0.5
    freq = np.concatenate([freq[0::2], freq[1::2]])
    angle = 2.0 * np.pi * np.outer(np.arange(BLOCK), freq) / (2 * BLOCK)
    forward = np.concatenate([np.cos(angle), -np.sin(angle)], axis=1)
    inverse = np.concatenate([np.cos(angle).T, -np.sin(angle).T], axis=0) * (scale / BLOCK)
    high = forward.astype(ml_dtypes.bfloat16)
    low = (forward - high.astype(np.float64)).astype(ml_dtypes.bfloat16)
    return high, low, inverse.astype(ml_dtypes.bfloat16)


def dot(left, right):
    return jnp.dot(left, right, preferred_element_type=jnp.float32)


def total(terms):
    real, imag = terms[0]
    for more_real, more_imag in terms[1:]:
        real, imag = real + more_real, imag + more_imag
    return real, imag


def times(left, right):
    return left[0] * right[0] - left[1] * right[1], left[0] * right[1] + left[1] * right[0]


def times_conj(left, right):
    return left[0] * right[0] + left[1] * right[1], left[1] * right[0] - left[0] * right[1]


def place():
    me = lax.axis_index("seq")
    return me // 2, me % 2


def forward(block, high_ref, low_ref):
    return dot(block, high_ref[...]) + dot(block, low_ref[...])


def tiles(chans, body):
    tile = 16 if chans % 16 == 0 else chans

    def step(i, carry):
        rows = pl.ds(pl.multiple_of(i * tile, tile), tile)
        for half in range(BLOCK // LANES):
            sign = 1.0 if half < BLOCK // LANES // 2 else -1.0
            body(rows, pl.ds(half * LANES, LANES), pl.ds(BLOCK + half * LANES, LANES), sign)
        return carry

    lax.fori_loop(0, chans // tile, step, 0, unroll=True)


def spectrum(ref, rows, re, im, *at):
    return ref[(*at, rows, re)], ref[(*at, rows, im)]


def convolved(c, signal, taps):
    return [times(signal[a], taps[c - a]) for a in signal if a <= c]


def correlated(c, signal, other):
    return [times_conj(signal[a], other[a - c]) for a in signal if a >= c]


def plus(left, right, sign):
    return left + right if sign > 0 else left - right


def put_convolution(sums, sign, put):
    for c in range(len(sums)):
        here, before = sums[c], sums[c - 1]
        put(c, here if c == 0 else (plus(here[0], before[1], -sign), plus(here[1], before[0], sign)))


def put_correlation(sums, sign, put):
    for c in range(len(sums)):
        here = sums[c]
        if c + 1 < len(sums):
            here = plus(here[0], sums[c + 1][1], sign), plus(here[1], sums[c + 1][0], -sign)
        put(c, here)


def putter(prod, rows, re, im):
    def put(c, value):
        prod[c, rows, re] = value[0].astype(jnp.bfloat16)
        prod[c, rows, im] = value[1].astype(jnp.bfloat16)

    return put


def gate_kernel(*refs):
    sources, held, (own_ref, other_ref, sems) = refs[:4], refs[4:8], refs[8:]
    chip, core = place()
    copies = [pltpu.make_async_copy(a, b, sems.at[i]) for i, (a, b) in enumerate(zip(sources, held))]
    for copy in copies:
        copy.start()
    for i in range(2):
        left, right = held[2 * i], held[2 * i + 1]
        copies[2 * i].wait()
        copies[2 * i + 1].wait()
        for k in range(own_ref.shape[0]):
            mine, theirs = 2 * (chip ^ k) + core, 2 * (chip ^ k) + 1 - core
            own_ref[k, i] = left[mine] * right[mine]
            other_ref[k, i] = left[theirs] * right[theirs]


def early(count):
    return [0, 3] if count == 4 else []


def late(count):
    return [k for k in range(count) if k not in early(count)]


def on_cases(count, work):
    if count != 4:
        return work((), tuple(range(count)))
    chip, _ = place()
    for ahead, rest in (((0, 3), (1, 2)), ((1, 2), (0, 3))):

        @pl.when((chip == ahead[0]) | (chip == ahead[1]))
        def _():
            work(ahead, rest)


def early_at(a):
    return jnp.where(place()[0] == a, 0, 1)


def late_at(a, count):
    return jnp.where(place()[0] ^ 1 == a, 0, 1) if count == 4 else a


def pieces_of(refs, count, chips):
    pieces, at = [], 0
    for k in chips:
        if k == 0:
            pieces.append((k, (refs[at].at[0], refs[at + 1].at[0])))
        elif k in early(count):
            pieces.append((k, (refs[at], refs[at + 1])))
        else:
            pieces.append((k, (refs[at].at[0], refs[at].at[1])))
        at += 2 if k == 0 or k in early(count) else 1
    return pieces, refs[at:]


def transform(pair, i, high_ref, low_ref):
    chip, core = place()
    mine, theirs = pair[0][i], pair[1][i]
    halves = [jnp.where(core == 0, mine, theirs), jnp.where(core == 0, theirs, mine)]
    return forward(jnp.concatenate(halves, axis=1), high_ref, low_ref)


def early_kernel(count, *refs):
    pieces, refs = pieces_of(refs, count, early(count))
    taps_ref, high_ref, low_ref, filt_ref, *refs = refs
    for a in range(count):
        filt_ref[a] = forward(taps_ref[:, a * BLOCK : (a + 1) * BLOCK], high_ref, low_ref)
    if not pieces:
        return
    wave_ref, conv_ref, back_ref = refs
    for at, (_, pair) in enumerate(pieces):
        for i in range(2):
            wave_ref[at, i] = transform(pair, i, high_ref, low_ref)

    def work(ahead, rest):
        def body(rows, re, im, sign):
            taps = [spectrum(filt_ref, rows, re, im, a) for a in range(count)]
            mixed, pulled = ({a: spectrum(wave_ref, rows, re, im, early_at(a), i) for a in ahead} for i in range(2))
            for c in range(count):
                for ref, terms in ((conv_ref, convolved(c, mixed, taps)), (back_ref, correlated(c, pulled, taps))):
                    if terms:
                        ref[c, rows, re], ref[c, rows, im] = total(terms)

        tiles(filt_ref.shape[1], body)

    on_cases(count, work)


def sides_kernel(count, *refs):
    pieces, refs = pieces_of(refs, count, late(count))
    filt_ref, high_ref, low_ref, inv_ref, *refs = refs
    parts, (own_ref, other_ref, wave_ref, prod) = refs[:-4], refs[-4:]
    chip, core = place()
    for at, (k, pair) in enumerate(pieces):
        for i in range(2):
            wave_ref[at if early(count) else chip ^ k, i] = transform(pair, i, high_ref, low_ref)

    def work(ahead, rest):
        def body(rows, re, im, sign):
            taps = [spectrum(filt_ref, rows, re, im, a) for a in range(count)]

            def sums(i, terms, has_part):
                signal = {a: spectrum(wave_ref, rows, re, im, late_at(a, count), i) for a in rest}
                begun = [[spectrum(parts[i], rows, re, im, c)] if has_part(c) else [] for c in range(count)]
                return [total(begun[c] + terms(c, signal, taps)) for c in range(count)]

            conv = sums(0, convolved, lambda c: any(a <= c for a in ahead))
            put_convolution(conv, sign, putter(prod.at[0], rows, re, im))
            back = sums(1, correlated, lambda c: any(a >= c for a in ahead))
            put_correlation(back, sign, putter(prod.at[1], rows, re, im))

        tiles(filt_ref.shape[1], body)

    on_cases(count, work)
    for k in range(count):
        for i in range(2):
            result = dot(prod[i, chip ^ k], inv_ref[...]).astype(jnp.bfloat16)
            first, second = result[:, :LANES], result[:, LANES:]
            own_ref[k, i] = jnp.where(core == 0, first, second)
            other_ref[k, i] = jnp.where(core == 0, second, first)


def reversed_bits(number, size):
    bits = size.bit_length() - 1
    return sum((number // 2**i % 2) * 2 ** (bits - 1 - i) for i in range(bits))


def lag_kernel(count, *refs):
    *early_refs, late_ref, inv_ref, lag_ref, prod = refs
    width = lag_ref.shape[2]
    slot = lax.axis_index("chan")

    def work(ahead, rest):
        def body(rows, re, im, sign):
            mixed, pulled = (
                {a: spectrum(early_refs[0], rows, re, im, early_at(a), i) for a in ahead}
                | {a: spectrum(late_ref, rows, re, im, late_at(a, count), i) for a in rest}
                for i in range(2)
            )
            sums = [total(correlated(c, pulled, mixed)) for c in range(count)]
            put_correlation(sums, sign, putter(prod, rows, re, im))

        tiles(prod.shape[1], body)

    on_cases(count, work)
    for c in range(prod.shape[0]):
        result = dot(prod[c], inv_ref[...]).astype(jnp.bfloat16)
        for u in range(BLOCK // LANES):
            begin = c * BLOCK + u * LANES
            at = reversed_bits(slot ^ (begin // width), lag_ref.shape[0])
            lag_ref[at, :, begin % width : begin % width + LANES] = result[:, u * LANES : (u + 1) * LANES]


def grads_kernel(count, *refs):
    rows_refs = refs[:count][::-1]
    query_ref, key_ref, value_ref, upstream_ref, kept_ref, sum_ref, *outs = refs[count:-5]
    filter_out, held, sems, sums, sum_sem = refs[-5:]
    chip, core = place()
    sums[...] = kept_ref[0].astype(jnp.float32) + sum_ref[0].astype(jnp.float32)
    copies = [pltpu.make_async_copy(sums, filter_out, sum_sem)]
    copies[0].start()
    for k in range(count):
        there = 2 * (chip ^ k)
        for at in range(2):
            group = there + at
            conv, back = rows_refs[k][core ^ at, 0], rows_refs[k][core ^ at, 1]
            held[0, 2 * k + at] = conv * query_ref[group]
            held[1, 2 * k + at] = conv * upstream_ref[group]
            held[2, 2 * k + at] = back * value_ref[group]
            held[3, 2 * k + at] = back * key_ref[group]
        for i, out in enumerate(outs):
            copy = pltpu.make_async_copy(held.at[i, pl.ds(2 * k, 2)], out.at[pl.ds(there, 2)], sems.at[i, k])
            copy.start()
            copies.append(copy)
    for copy in copies:
        copy.wait()


VMEM = pl.BlockSpec(memory_space=pltpu.VMEM)
ANY = pl.BlockSpec(memory_space=pl.ANY)
HBM = pl.BlockSpec(memory_space=pltpu.HBM)
LIMIT = 16 * 1024 * 1024


def call(kernel, args, outs, scratch, name, space=VMEM, out_space=VMEM, after=(), flops=0):
    def body(*refs):
        kernel(*refs[: len(args)], *refs[len(args) + len(after) :])

    return pl.pallas_call(
        body,
        out_shape=tuple(jax.ShapeDtypeStruct(shape, kind) for shape, kind in outs),
        in_specs=[space] * len(args) + [ANY] * len(after),
        out_specs=(out_space,) * len(outs),
        scratch_shapes=scratch,
        compiler_params=pltpu.CompilerParams(vmem_limit_bytes=LIMIT),
        cost_estimate=pl.CostEstimate(flops=flops, bytes_accessed=0, transcendentals=0) if flops else None,
        name=name,
    )(*args, *after)


def swap(array, axis, k):
    return lax.ppermute(array, axis, [(i, i ^ k) for i in range(lax.axis_size(axis))])


def exchange(own, other, ahead):
    count = own.shape[0]
    got = swap(other, "seq", 1)
    first = [own, got]
    for k in ahead:
        first += [swap(own[k], "seq", 2 * k), swap(got[k], "seq", 2 * k)]
    rest = [k for k in reversed(range(1, count)) if k not in ahead]
    return first, [swap(jnp.stack([own[k], got[k]]), "seq", 2 * k) for k in rest]


def scatter_sum(pieces):
    size, step = pieces.shape[0], 1
    while True:
        kept, sent = pieces[: size // 2], pieces[size // 2 :].astype(jnp.bfloat16)
        got = swap(sent, "chan", step)
        if size == 2:
            return kept, got
        pieces = kept.astype(jnp.float32) + got.astype(jnp.float32)
        size, step = size // 2, step * 2


def on_device(query, key, value, upstream, taps):
    seq, chan = lax.axis_size("seq"), lax.axis_size("chan")
    wide, positions = query.shape
    chans, length = taps.shape
    count = seq // 2
    query, key, value, upstream = (x.reshape(seq, chans, positions) for x in (query, key, value, upstream))
    high, low, inverse = (jnp.asarray(x) for x in transform_tables(1.0 / math.sqrt(length)))
    half = ((count, 2, chans, positions), jnp.bfloat16)
    whole = ((seq, chans, positions), jnp.bfloat16)
    wave = ((count, chans, 2 * BLOCK), jnp.float32)
    key, value, upstream, query, own, other = call(
        gate_kernel,
        tuple(pltpu.with_memory_space_constraint(x, pltpu.HBM) for x in (key, value, upstream, query)),
        (whole,) * 4 + (half,) * 2,
        [pltpu.SemaphoreType.DMA((4,))],
        "gate",
        HBM,
    )
    first, rest = exchange(own, other, early(count)[1:])
    rest = rest[::-1]
    if not early(count):
        first, rest = [], first + rest
    waves = ((len(early(count)), 2, chans, 2 * BLOCK), jnp.float32)
    filt, *begun = call(
        functools.partial(early_kernel, count),
        (*first, taps, high, low),
        (wave, *((waves, wave, wave) if early(count) else ())),
        [],
        "early",
        flops=int(2e9),
    )
    waves = ((len(late(count)), 2, chans, 2 * BLOCK), jnp.float32)
    prod = pltpu.VMEM((count, chans, 2 * BLOCK), jnp.bfloat16)
    own, other, late_waves = call(
        functools.partial(sides_kernel, count),
        (*rest, filt, high, low, inverse, *begun[1:]),
        (half, half, waves),
        [pltpu.VMEM((2, count, chans, 2 * BLOCK), jnp.bfloat16)],
        "sides",
    )
    stay, rows = exchange(own, other, [])
    pieces = ((chan, chans, length // chan), jnp.bfloat16)
    (lag,) = call(
        functools.partial(lag_kernel, count),
        (*begun[:1], late_waves, inverse),
        (pieces,),
        [prod],
        "lag",
        after=(own,),
    )
    lag, _ = lax.optimization_barrier((lag, stay[1]))
    kept, got = scatter_sum(lag)
    sums = ((chans, length // chan), jnp.float32)
    *outs, filter_grad = call(
        functools.partial(grads_kernel, count),
        (*rows, jnp.stack([stay[0][0], stay[1][0]]), query, key, value, upstream, kept, got),
        (whole,) * 4 + (sums,),
        [
            pltpu.VMEM((4, seq, chans, positions), jnp.bfloat16),
            pltpu.SemaphoreType.DMA((4, count)),
            pltpu.VMEM(*sums),
            pltpu.SemaphoreType.DMA,
        ],
        "grads",
        out_space=HBM,
    )
    return (*(x.reshape(wide, positions) for x in outs), filter_grad)


def solution(mesh):
    block = P("chan", "seq")
    return jax.shard_map(
        on_device,
        mesh=mesh,
        in_specs=(block, block, block, block, P("seq", None)),
        out_specs=(block, block, block, block, P("seq", "chan")),
        check_vma=False,
    )
```

```python
import functools
import math

import jax
import jax.numpy as jnp
import ml_dtypes
import numpy as np
from jax import lax
from jax.experimental import pallas as pl
from jax.experimental.pallas import tpu as pltpu
from jax.sharding import PartitionSpec as P

BLOCK = 256
LANES = 128


def transform_tables(scale):
    freq = np.arange(BLOCK) + 0.5
    freq = np.concatenate([freq[0::2], freq[1::2]])
    angle = 2.0 * np.pi * np.outer(np.arange(BLOCK), freq) / (2 * BLOCK)
    forward = np.concatenate([np.cos(angle), -np.sin(angle)], axis=1)
    inverse = np.concatenate([np.cos(angle).T, -np.sin(angle).T], axis=0) * (scale / BLOCK)
    high = forward.astype(ml_dtypes.bfloat16)
    low = (forward - high.astype(np.float64)).astype(ml_dtypes.bfloat16)
    return high, low, inverse.astype(ml_dtypes.bfloat16)


def dot(left, right):
    return jnp.dot(left, right, preferred_element_type=jnp.float32)


def total(terms):
    real, imag = terms[0]
    for more_real, more_imag in terms[1:]:
        real, imag = real + more_real, imag + more_imag
    return real, imag


def times(left, right):
    return left[0] * right[0] - left[1] * right[1], left[0] * right[1] + left[1] * right[0]


def times_conj(left, right):
    return left[0] * right[0] + left[1] * right[1], left[1] * right[0] - left[0] * right[1]


def place():
    me = lax.axis_index("seq")
    return me // 2, me % 2


def forward(block, high_ref, low_ref):
    return dot(block, high_ref[...]) + dot(block, low_ref[...])


def tiles(chans, body):
    tile = 16 if chans % 16 == 0 else chans

    def step(i, carry):
        rows = pl.ds(pl.multiple_of(i * tile, tile), tile)
        for half in range(BLOCK // LANES):
            sign = 1.0 if half < BLOCK // LANES // 2 else -1.0
            body(rows, pl.ds(half * LANES, LANES), pl.ds(BLOCK + half * LANES, LANES), sign)
        return carry

    lax.fori_loop(0, chans // tile, step, 0, unroll=True)


def spectrum(ref, rows, re, im, *at):
    return ref[(*at, rows, re)], ref[(*at, rows, im)]


def convolved(c, signal, taps):
    return [times(signal[a], taps[c - a]) for a in signal if a <= c]


def correlated(c, signal, other):
    return [times_conj(signal[a], other[a - c]) for a in signal if a >= c]


def plus(left, right, sign):
    return left + right if sign > 0 else left - right


def put_convolution(sums, sign, put):
    for c in range(len(sums)):
        here, before = sums[c], sums[c - 1]
        put(c, here if c == 0 else (plus(here[0], before[1], -sign), plus(here[1], before[0], sign)))


def put_correlation(sums, sign, put):
    for c in range(len(sums)):
        here = sums[c]
        if c + 1 < len(sums):
            here = plus(here[0], sums[c + 1][1], sign), plus(here[1], sums[c + 1][0], -sign)
        put(c, here)


def putter(prod, rows, re, im):
    def put(c, value):
        prod[c, rows, re] = value[0].astype(jnp.bfloat16)
        prod[c, rows, im] = value[1].astype(jnp.bfloat16)

    return put


def gate_kernel(*refs):
    sources, held, (own_ref, other_ref, sems) = refs[:4], refs[4:8], refs[8:]
    chip, core = place()
    copies = [pltpu.make_async_copy(a, b, sems.at[i]) for i, (a, b) in enumerate(zip(sources, held))]
    for copy in copies:
        copy.start()
    for i in range(2):
        left, right = held[2 * i], held[2 * i + 1]
        copies[2 * i].wait()
        copies[2 * i + 1].wait()
        for k in range(own_ref.shape[0]):
            mine, theirs = 2 * (chip ^ k) + core, 2 * (chip ^ k) + 1 - core
            own_ref[k, i] = left[mine] * right[mine]
            other_ref[k, i] = left[theirs] * right[theirs]


def early(count):
    return [0, 3] if count == 4 else []


def late(count):
    return [k for k in range(count) if k not in early(count)]


def on_cases(count, work):
    if count != 4:
        return work((), tuple(range(count)))
    chip, _ = place()
    for ahead, rest in (((0, 3), (1, 2)), ((1, 2), (0, 3))):

        @pl.when((chip == ahead[0]) | (chip == ahead[1]))
        def _():
            work(ahead, rest)


def early_at(a):
    return jnp.where(place()[0] == a, 0, 1)


def late_at(a, count):
    return jnp.where(place()[0] ^ 1 == a, 0, 1) if count == 4 else a


def pieces_of(refs, count, chips):
    pieces, at = [], 0
    for k in chips:
        if k == 0:
            pieces.append((k, (refs[at].at[0], refs[at + 1].at[0])))
        elif k in early(count):
            pieces.append((k, (refs[at], refs[at + 1])))
        else:
            pieces.append((k, (refs[at].at[0], refs[at].at[1])))
        at += 2 if k == 0 or k in early(count) else 1
    return pieces, refs[at:]


def transform(pair, i, high_ref, low_ref):
    chip, core = place()
    mine, theirs = pair[0][i], pair[1][i]
    halves = [jnp.where(core == 0, mine, theirs), jnp.where(core == 0, theirs, mine)]
    return forward(jnp.concatenate(halves, axis=1), high_ref, low_ref)


def early_kernel(count, *refs):
    pieces, refs = pieces_of(refs, count, early(count))
    taps_ref, high_ref, low_ref, filt_ref, *refs = refs
    for a in range(count):
        filt_ref[a] = forward(taps_ref[:, a * BLOCK : (a + 1) * BLOCK], high_ref, low_ref)
    if not pieces:
        return
    wave_ref, conv_ref, back_ref = refs
    for at, (_, pair) in enumerate(pieces):
        for i in range(2):
            wave_ref[at, i] = transform(pair, i, high_ref, low_ref)

    def work(ahead, rest):
        def body(rows, re, im, sign):
            taps = [spectrum(filt_ref, rows, re, im, a) for a in range(count)]
            mixed, pulled = ({a: spectrum(wave_ref, rows, re, im, early_at(a), i) for a in ahead} for i in range(2))
            for c in range(count):
                for ref, terms in ((conv_ref, convolved(c, mixed, taps)), (back_ref, correlated(c, pulled, taps))):
                    if terms:
                        ref[c, rows, re], ref[c, rows, im] = total(terms)

        tiles(filt_ref.shape[1], body)

    on_cases(count, work)


def sides_kernel(count, *refs):
    pieces, refs = pieces_of(refs, count, late(count))
    filt_ref, high_ref, low_ref, inv_ref, *refs = refs
    parts, (own_ref, other_ref, wave_ref, prod) = refs[:-4], refs[-4:]
    chip, core = place()
    for at, (k, pair) in enumerate(pieces):
        for i in range(2):
            wave_ref[at if early(count) else chip ^ k, i] = transform(pair, i, high_ref, low_ref)

    def work(ahead, rest):
        def body(rows, re, im, sign):
            taps = [spectrum(filt_ref, rows, re, im, a) for a in range(count)]

            def sums(i, terms, has_part):
                signal = {a: spectrum(wave_ref, rows, re, im, late_at(a, count), i) for a in rest}
                begun = [[spectrum(parts[i], rows, re, im, c)] if has_part(c) else [] for c in range(count)]
                return [total(begun[c] + terms(c, signal, taps)) for c in range(count)]

            conv = sums(0, convolved, lambda c: any(a <= c for a in ahead))
            put_convolution(conv, sign, putter(prod.at[0], rows, re, im))
            back = sums(1, correlated, lambda c: any(a >= c for a in ahead))
            put_correlation(back, sign, putter(prod.at[1], rows, re, im))

        tiles(filt_ref.shape[1], body)

    on_cases(count, work)
    for k in range(count):
        for i in range(2):
            result = dot(prod[i, chip ^ k], inv_ref[...]).astype(jnp.bfloat16)
            first, second = result[:, :LANES], result[:, LANES:]
            own_ref[k, i] = jnp.where(core == 0, first, second)
            other_ref[k, i] = jnp.where(core == 0, second, first)


def reversed_bits(number, size):
    bits = size.bit_length() - 1
    return sum((number // 2**i % 2) * 2 ** (bits - 1 - i) for i in range(bits))


def lag_kernel(count, *refs):
    *early_refs, late_ref, inv_ref, lag_ref, prod = refs
    width = lag_ref.shape[2]
    slot = lax.axis_index("chan")

    def work(ahead, rest):
        def body(rows, re, im, sign):
            mixed, pulled = (
                {a: spectrum(early_refs[0], rows, re, im, early_at(a), i) for a in ahead}
                | {a: spectrum(late_ref, rows, re, im, late_at(a, count), i) for a in rest}
                for i in range(2)
            )
            sums = [total(correlated(c, pulled, mixed)) for c in range(count)]
            put_correlation(sums, sign, putter(prod, rows, re, im))

        tiles(prod.shape[1], body)

    on_cases(count, work)
    for c in range(prod.shape[0]):
        result = dot(prod[c], inv_ref[...]).astype(jnp.bfloat16)
        for u in range(BLOCK // LANES):
            begin = c * BLOCK + u * LANES
            at = reversed_bits(slot ^ (begin // width), lag_ref.shape[0])
            lag_ref[at, :, begin % width : begin % width + LANES] = result[:, u * LANES : (u + 1) * LANES]


def grads_kernel(count, *refs):
    rows_refs = refs[:count][::-1]
    query_ref, key_ref, value_ref, upstream_ref, *term_refs = refs[count:-9]
    outs, (filter_out, held, sems, sums, sum_sem) = refs[-9:-5], refs[-5:]
    chip, core = place()
    sums[...] = sum(ref[0].astype(jnp.float32) for ref in term_refs)
    copies = [pltpu.make_async_copy(sums, filter_out, sum_sem)]
    copies[0].start()
    for k in range(count):
        there = 2 * (chip ^ k)
        for at in range(2):
            group = there + at
            conv, back = rows_refs[k][core ^ at, 0], rows_refs[k][core ^ at, 1]
            held[0, 2 * k + at] = conv * query_ref[group]
            held[1, 2 * k + at] = conv * upstream_ref[group]
            held[2, 2 * k + at] = back * value_ref[group]
            held[3, 2 * k + at] = back * key_ref[group]
        for i, out in enumerate(outs):
            copy = pltpu.make_async_copy(held.at[i, pl.ds(2 * k, 2)], out.at[pl.ds(there, 2)], sems.at[i, k])
            copy.start()
            copies.append(copy)
    for copy in copies:
        copy.wait()


VMEM = pl.BlockSpec(memory_space=pltpu.VMEM)
ANY = pl.BlockSpec(memory_space=pl.ANY)
HBM = pl.BlockSpec(memory_space=pltpu.HBM)
LIMIT = 16 * 1024 * 1024


def call(kernel, args, outs, scratch, name, space=VMEM, out_space=VMEM, after=(), flops=0):
    def body(*refs):
        kernel(*refs[: len(args)], *refs[len(args) + len(after) :])

    return pl.pallas_call(
        body,
        out_shape=tuple(jax.ShapeDtypeStruct(shape, kind) for shape, kind in outs),
        in_specs=[space] * len(args) + [ANY] * len(after),
        out_specs=(out_space,) * len(outs),
        scratch_shapes=scratch,
        compiler_params=pltpu.CompilerParams(vmem_limit_bytes=LIMIT),
        cost_estimate=pl.CostEstimate(flops=flops, bytes_accessed=0, transcendentals=0) if flops else None,
        name=name,
    )(*args, *after)


def swap(array, axis, k):
    return lax.ppermute(array, axis, [(i, i ^ k) for i in range(lax.axis_size(axis))])


def exchange(own, other, ahead):
    count = own.shape[0]
    got = swap(other, "seq", 1)
    first = [own, got]
    for k in ahead:
        first += [swap(own[k], "seq", 2 * k), swap(got[k], "seq", 2 * k)]
    rest = [k for k in reversed(range(1, count)) if k not in ahead]
    return first, [swap(jnp.stack([own[k], got[k]]), "seq", 2 * k) for k in rest]


def scatter_sum(pieces, behind):
    size, step = pieces.shape[0], 1
    if size == 4:
        passed = swap(pieces[3:], "chan", 1)
        stays = swap(pieces[2:3], "chan", 1)
        onward = pieces[1:2].astype(jnp.float32) + passed.astype(jnp.float32)
        return [pieces[:1], stays, swap(onward.astype(jnp.bfloat16), "chan", 2)]
    while size > 2:
        kept, sent = pieces[: size // 2], pieces[size // 2 :].astype(jnp.bfloat16)
        pieces = kept.astype(jnp.float32) + swap(sent, "chan", step).astype(jnp.float32)
        size, step = size // 2, step * 2
    return [pieces[:1], swap(pieces[1:].astype(jnp.bfloat16), "chan", step)]


def on_device(query, key, value, upstream, taps):
    seq, chan = lax.axis_size("seq"), lax.axis_size("chan")
    wide, positions = query.shape
    chans, length = taps.shape
    count = seq // 2
    query, key, value, upstream = (x.reshape(seq, chans, positions) for x in (query, key, value, upstream))
    high, low, inverse = (jnp.asarray(x) for x in transform_tables(1.0 / math.sqrt(length)))
    half = ((count, 2, chans, positions), jnp.bfloat16)
    whole = ((seq, chans, positions), jnp.bfloat16)
    wave = ((count, chans, 2 * BLOCK), jnp.float32)
    key, value, upstream, query, own, other = call(
        gate_kernel,
        tuple(pltpu.with_memory_space_constraint(x, pltpu.HBM) for x in (key, value, upstream, query)),
        (whole,) * 4 + (half,) * 2,
        [pltpu.SemaphoreType.DMA((4,))],
        "gate",
        HBM,
    )
    first, rest = exchange(own, other, early(count)[1:])
    rest = rest[::-1]
    if not early(count):
        first, rest = [], first + rest
    waves = ((len(early(count)), 2, chans, 2 * BLOCK), jnp.float32)
    filt, *begun = call(
        functools.partial(early_kernel, count),
        (*first, taps, high, low),
        (wave, *((waves, wave, wave) if early(count) else ())),
        [],
        "early",
        flops=int(2e9),
    )
    waves = ((len(late(count)), 2, chans, 2 * BLOCK), jnp.float32)
    prod = pltpu.VMEM((count, chans, 2 * BLOCK), jnp.bfloat16)
    own, other, late_waves = call(
        functools.partial(sides_kernel, count),
        (*rest, filt, high, low, inverse, *begun[1:]),
        (half, half, waves),
        [pltpu.VMEM((2, count, chans, 2 * BLOCK), jnp.bfloat16)],
        "sides",
    )
    stay, rows = exchange(own, other, [])
    pieces = ((chan, chans, length // chan), jnp.bfloat16)
    (lag,) = call(
        functools.partial(lag_kernel, count),
        (*begun[:1], late_waves, inverse),
        (pieces,),
        [prod],
        "lag",
        after=(own,),
    )
    terms = scatter_sum(lag, stay[1])
    sums = ((chans, length // chan), jnp.float32)
    *outs, filter_grad = call(
        functools.partial(grads_kernel, count),
        (*rows, jnp.stack([stay[0][0], stay[1][0]]), query, key, value, upstream, *terms),
        (whole,) * 4 + (sums,),
        [
            pltpu.VMEM((4, seq, chans, positions), jnp.bfloat16),
            pltpu.SemaphoreType.DMA((4, count)),
            pltpu.VMEM(*sums),
            pltpu.SemaphoreType.DMA,
        ],
        "grads",
        out_space=HBM,
    )
    return (*(x.reshape(wide, positions) for x in outs), filter_grad)


def solution(mesh):
    block = P("chan", "seq")
    return jax.shard_map(
        on_device,
        mesh=mesh,
        in_specs=(block, block, block, block, P("seq", None)),
        out_specs=(block, block, block, block, P("seq", "chan")),
        check_vma=False,
    )
```

```python
import functools
import math

import jax
import jax.numpy as jnp
import ml_dtypes
import numpy as np
from jax import lax
from jax.experimental import pallas as pl
from jax.experimental.pallas import tpu as pltpu
from jax.sharding import PartitionSpec as P

BLOCK = 256
LANES = 128


def transform_tables(scale):
    freq = np.arange(BLOCK) + 0.5
    freq = np.concatenate([freq[0::2], freq[1::2]])
    angle = 2.0 * np.pi * np.outer(np.arange(BLOCK), freq) / (2 * BLOCK)
    forward = np.concatenate([np.cos(angle), -np.sin(angle)], axis=1)
    inverse = np.concatenate([np.cos(angle).T, -np.sin(angle).T], axis=0) * (scale / BLOCK)
    high = forward.astype(ml_dtypes.bfloat16)
    low = (forward - high.astype(np.float64)).astype(ml_dtypes.bfloat16)
    return high, low, inverse.astype(ml_dtypes.bfloat16)


def dot(left, right):
    return jnp.dot(left, right, preferred_element_type=jnp.float32)


def total(terms):
    real, imag = terms[0]
    for more_real, more_imag in terms[1:]:
        real, imag = real + more_real, imag + more_imag
    return real, imag


def times(left, right):
    return left[0] * right[0] - left[1] * right[1], left[0] * right[1] + left[1] * right[0]


def times_conj(left, right):
    return left[0] * right[0] + left[1] * right[1], left[1] * right[0] - left[0] * right[1]


def place():
    me = lax.axis_index("seq")
    return me // 2, me % 2


def forward(block, high_ref, low_ref):
    return dot(block, high_ref[...]) + dot(block, low_ref[...])


def tiles(chans, body):
    tile = 16 if chans % 16 == 0 else chans

    def step(i, carry):
        rows = pl.ds(pl.multiple_of(i * tile, tile), tile)
        for half in range(BLOCK // LANES):
            sign = 1.0 if half < BLOCK // LANES // 2 else -1.0
            body(rows, pl.ds(half * LANES, LANES), pl.ds(BLOCK + half * LANES, LANES), sign)
        return carry

    lax.fori_loop(0, chans // tile, step, 0, unroll=True)


def spectrum(ref, rows, re, im, *at):
    return ref[(*at, rows, re)], ref[(*at, rows, im)]


def convolved(c, signal, taps):
    return [times(signal[a], taps[c - a]) for a in signal if a <= c]


def correlated(c, signal, other):
    return [times_conj(signal[a], other[a - c]) for a in signal if a >= c]


def plus(left, right, sign):
    return left + right if sign > 0 else left - right


def put_convolution(sums, sign, put):
    for c in range(len(sums)):
        here, before = sums[c], sums[c - 1]
        put(c, here if c == 0 else (plus(here[0], before[1], -sign), plus(here[1], before[0], sign)))


def put_correlation(sums, sign, put):
    for c in range(len(sums)):
        here = sums[c]
        if c + 1 < len(sums):
            here = plus(here[0], sums[c + 1][1], sign), plus(here[1], sums[c + 1][0], -sign)
        put(c, here)


def putter(prod, rows, re, im):
    def put(c, value):
        prod[c, rows, re] = value[0].astype(jnp.bfloat16)
        prod[c, rows, im] = value[1].astype(jnp.bfloat16)

    return put


def gate_kernel(*refs):
    sources, held, (own_ref, other_ref, sems) = refs[:4], refs[4:8], refs[8:]
    chip, core = place()
    copies = [pltpu.make_async_copy(a, b, sems.at[i]) for i, (a, b) in enumerate(zip(sources, held))]
    for copy in copies:
        copy.start()
    for i in range(2):
        left, right = held[2 * i], held[2 * i + 1]
        copies[2 * i].wait()
        copies[2 * i + 1].wait()
        for k in range(own_ref.shape[0]):
            mine, theirs = 2 * (chip ^ k) + core, 2 * (chip ^ k) + 1 - core
            own_ref[k, i] = left[mine] * right[mine]
            other_ref[k, i] = left[theirs] * right[theirs]


def early(count):
    return [0, 3] if count == 4 else []


def late(count):
    return [k for k in range(count) if k not in early(count)]


def on_cases(count, work):
    if count != 4:
        return work((), tuple(range(count)))
    chip, _ = place()
    for ahead, rest in (((0, 3), (1, 2)), ((1, 2), (0, 3))):

        @pl.when((chip == ahead[0]) | (chip == ahead[1]))
        def _():
            work(ahead, rest)


def early_at(a):
    return jnp.where(place()[0] == a, 0, 1)


def late_at(a, count):
    return jnp.where(place()[0] ^ 1 == a, 0, 1) if count == 4 else a


def pieces_of(refs, count, chips):
    pieces, at = [], 0
    for k in chips:
        if k == 0:
            pieces.append((k, (refs[at].at[0], refs[at + 1].at[0])))
        elif k in early(count):
            pieces.append((k, (refs[at], refs[at + 1])))
        else:
            pieces.append((k, (refs[at].at[0], refs[at].at[1])))
        at += 2 if k == 0 or k in early(count) else 1
    return pieces, refs[at:]


def transform(pair, i, high_ref, low_ref):
    chip, core = place()
    mine, theirs = pair[0][i], pair[1][i]
    halves = [jnp.where(core == 0, mine, theirs), jnp.where(core == 0, theirs, mine)]
    return forward(jnp.concatenate(halves, axis=1), high_ref, low_ref)


def early_kernel(count, *refs):
    pieces, refs = pieces_of(refs, count, early(count))
    taps_ref, high_ref, low_ref, filt_ref, *refs = refs
    for a in range(count):
        filt_ref[a] = forward(taps_ref[:, a * BLOCK : (a + 1) * BLOCK], high_ref, low_ref)
    if not pieces:
        return
    wave_ref, conv_ref, back_ref = refs
    for at, (_, pair) in enumerate(pieces):
        for i in range(2):
            wave_ref[at, i] = transform(pair, i, high_ref, low_ref)

    def work(ahead, rest):
        def body(rows, re, im, sign):
            taps = [spectrum(filt_ref, rows, re, im, a) for a in range(count)]
            mixed, pulled = ({a: spectrum(wave_ref, rows, re, im, early_at(a), i) for a in ahead} for i in range(2))
            for c in range(count):
                for ref, terms in ((conv_ref, convolved(c, mixed, taps)), (back_ref, correlated(c, pulled, taps))):
                    if terms:
                        ref[c, rows, re], ref[c, rows, im] = total(terms)

        tiles(filt_ref.shape[1], body)

    on_cases(count, work)


def next_kernel(part_ref, high_ref, low_ref, wave_ref):
    for i in range(2):
        wave_ref[i] = transform((part_ref.at[0], part_ref.at[1]), i, high_ref, low_ref)


def sides_kernel(count, *refs):
    done = refs[:1] if early(count) else ()
    pieces, refs = pieces_of(refs[len(done) :], count, late(count)[len(done) :])
    filt_ref, high_ref, low_ref, inv_ref, *refs = refs
    parts, (own_ref, other_ref, wave_ref, prod) = refs[:-4], refs[-4:]
    chip, core = place()
    for ref in done:
        wave_ref[0] = ref[...]
    for at, (k, pair) in enumerate(pieces, len(done)):
        for i in range(2):
            wave_ref[at if early(count) else chip ^ k, i] = transform(pair, i, high_ref, low_ref)

    def work(ahead, rest):
        def body(rows, re, im, sign):
            taps = [spectrum(filt_ref, rows, re, im, a) for a in range(count)]

            def sums(i, terms, has_part):
                signal = {a: spectrum(wave_ref, rows, re, im, late_at(a, count), i) for a in rest}
                begun = [[spectrum(parts[i], rows, re, im, c)] if has_part(c) else [] for c in range(count)]
                return [total(begun[c] + terms(c, signal, taps)) for c in range(count)]

            conv = sums(0, convolved, lambda c: any(a <= c for a in ahead))
            put_convolution(conv, sign, putter(prod.at[0], rows, re, im))
            back = sums(1, correlated, lambda c: any(a >= c for a in ahead))
            put_correlation(back, sign, putter(prod.at[1], rows, re, im))

        tiles(filt_ref.shape[1], body)

    on_cases(count, work)
    for k in range(count):
        for i in range(2):
            result = dot(prod[i, chip ^ k], inv_ref[...]).astype(jnp.bfloat16)
            first, second = result[:, :LANES], result[:, LANES:]
            own_ref[k, i] = jnp.where(core == 0, first, second)
            other_ref[k, i] = jnp.where(core == 0, second, first)


def reversed_bits(number, size):
    bits = size.bit_length() - 1
    return sum((number // 2**i % 2) * 2 ** (bits - 1 - i) for i in range(bits))


def lag_kernel(count, *refs):
    *early_refs, late_ref, inv_ref, lag_ref, prod = refs
    width = lag_ref.shape[2]
    slot = lax.axis_index("chan")

    def work(ahead, rest):
        def body(rows, re, im, sign):
            mixed, pulled = (
                {a: spectrum(early_refs[0], rows, re, im, early_at(a), i) for a in ahead}
                | {a: spectrum(late_ref, rows, re, im, late_at(a, count), i) for a in rest}
                for i in range(2)
            )
            sums = [total(correlated(c, pulled, mixed)) for c in range(count)]
            put_correlation(sums, sign, putter(prod, rows, re, im))

        tiles(prod.shape[1], body)

    on_cases(count, work)
    for c in range(prod.shape[0]):
        result = dot(prod[c], inv_ref[...]).astype(jnp.bfloat16)
        for u in range(BLOCK // LANES):
            begin = c * BLOCK + u * LANES
            at = reversed_bits(slot ^ (begin // width), lag_ref.shape[0])
            lag_ref[at, :, begin % width : begin % width + LANES] = result[:, u * LANES : (u + 1) * LANES]


def grads_kernel(count, *refs):
    rows_refs = refs[:count][::-1]
    query_ref, key_ref, value_ref, upstream_ref, *term_refs = refs[count:-9]
    outs, (filter_out, held, sems, sums, sum_sem) = refs[-9:-5], refs[-5:]
    chip, core = place()
    sums[...] = sum(ref[0].astype(jnp.float32) for ref in term_refs)
    copies = [pltpu.make_async_copy(sums, filter_out, sum_sem)]
    copies[0].start()
    for k in range(count):
        there = 2 * (chip ^ k)
        for at in range(2):
            group = there + at
            conv, back = rows_refs[k][core ^ at, 0], rows_refs[k][core ^ at, 1]
            held[0, 2 * k + at] = conv * query_ref[group]
            held[1, 2 * k + at] = conv * upstream_ref[group]
            held[2, 2 * k + at] = back * value_ref[group]
            held[3, 2 * k + at] = back * key_ref[group]
        for i, out in enumerate(outs):
            copy = pltpu.make_async_copy(held.at[i, pl.ds(2 * k, 2)], out.at[pl.ds(there, 2)], sems.at[i, k])
            copy.start()
            copies.append(copy)
    for copy in copies:
        copy.wait()


VMEM = pl.BlockSpec(memory_space=pltpu.VMEM)
ANY = pl.BlockSpec(memory_space=pl.ANY)
HBM = pl.BlockSpec(memory_space=pltpu.HBM)
LIMIT = 16 * 1024 * 1024


def call(kernel, args, outs, scratch, name, space=VMEM, out_space=VMEM, after=(), flops=0):
    def body(*refs):
        kernel(*refs[: len(args)], *refs[len(args) + len(after) :])

    return pl.pallas_call(
        body,
        out_shape=tuple(jax.ShapeDtypeStruct(shape, kind) for shape, kind in outs),
        in_specs=[space] * len(args) + [ANY] * len(after),
        out_specs=(out_space,) * len(outs),
        scratch_shapes=scratch,
        compiler_params=pltpu.CompilerParams(vmem_limit_bytes=LIMIT),
        cost_estimate=pl.CostEstimate(flops=flops, bytes_accessed=0, transcendentals=0) if flops else None,
        name=name,
    )(*args, *after)


def swap(array, axis, k):
    return lax.ppermute(array, axis, [(i, i ^ k) for i in range(lax.axis_size(axis))])


def exchange(own, other, ahead):
    count = own.shape[0]
    got = swap(other, "seq", 1)
    first = [own, got]
    for k in ahead:
        first += [swap(own[k], "seq", 2 * k), swap(got[k], "seq", 2 * k)]
    rest = [k for k in reversed(range(1, count)) if k not in ahead]
    return first, [swap(jnp.stack([own[k], got[k]]), "seq", 2 * k) for k in rest]


def scatter_sum(pieces, behind):
    size, step = pieces.shape[0], 1
    if size == 4:
        passed = swap(pieces[3:], "chan", 1)
        stays = swap(pieces[2:3], "chan", 1)
        onward = pieces[1:2].astype(jnp.float32) + passed.astype(jnp.float32)
        return [pieces[:1], stays, swap(onward.astype(jnp.bfloat16), "chan", 2)]
    while size > 2:
        kept, sent = pieces[: size // 2], pieces[size // 2 :].astype(jnp.bfloat16)
        pieces = kept.astype(jnp.float32) + swap(sent, "chan", step).astype(jnp.float32)
        size, step = size // 2, step * 2
    return [pieces[:1], swap(pieces[1:].astype(jnp.bfloat16), "chan", step)]


def on_device(query, key, value, upstream, taps):
    seq, chan = lax.axis_size("seq"), lax.axis_size("chan")
    wide, positions = query.shape
    chans, length = taps.shape
    count = seq // 2
    query, key, value, upstream = (x.reshape(seq, chans, positions) for x in (query, key, value, upstream))
    high, low, inverse = (jnp.asarray(x) for x in transform_tables(1.0 / math.sqrt(length)))
    half = ((count, 2, chans, positions), jnp.bfloat16)
    whole = ((seq, chans, positions), jnp.bfloat16)
    wave = ((count, chans, 2 * BLOCK), jnp.float32)
    key, value, upstream, query, own, other = call(
        gate_kernel,
        tuple(pltpu.with_memory_space_constraint(x, pltpu.HBM) for x in (key, value, upstream, query)),
        (whole,) * 4 + (half,) * 2,
        [pltpu.SemaphoreType.DMA((4,))],
        "gate",
        HBM,
    )
    first, rest = exchange(own, other, early(count)[1:])
    rest = rest[::-1]
    if not early(count):
        first, rest = [], first + rest
    waves = ((len(early(count)), 2, chans, 2 * BLOCK), jnp.float32)
    filt, *begun = call(
        functools.partial(early_kernel, count),
        (*first, taps, high, low),
        (wave, *((waves, wave, wave) if early(count) else ())),
        [],
        "early",
        flops=int(2e9),
    )
    waves = ((len(late(count)), 2, chans, 2 * BLOCK), jnp.float32)
    if early(count):
        rest[:1] = call(next_kernel, (rest[0], high, low), (((2, *waves[0][2:]), jnp.float32),), [], "next", flops=0)
    prod = pltpu.VMEM((count, chans, 2 * BLOCK), jnp.bfloat16)
    own, other, late_waves = call(
        functools.partial(sides_kernel, count),
        (*rest, filt, high, low, inverse, *begun[1:]),
        (half, half, waves),
        [pltpu.VMEM((2, count, chans, 2 * BLOCK), jnp.bfloat16)],
        "sides",
    )
    stay, rows = exchange(own, other, [])
    pieces = ((chan, chans, length // chan), jnp.bfloat16)
    (lag,) = call(
        functools.partial(lag_kernel, count),
        (*begun[:1], late_waves, inverse),
        (pieces,),
        [prod],
        "lag",
        after=(own,),
    )
    terms = scatter_sum(lag, stay[1])
    sums = ((chans, length // chan), jnp.float32)
    *outs, filter_grad = call(
        functools.partial(grads_kernel, count),
        (*rows, jnp.stack([stay[0][0], stay[1][0]]), query, key, value, upstream, *terms),
        (whole,) * 4 + (sums,),
        [
            pltpu.VMEM((4, seq, chans, positions), jnp.bfloat16),
            pltpu.SemaphoreType.DMA((4, count)),
            pltpu.VMEM(*sums),
            pltpu.SemaphoreType.DMA,
        ],
        "grads",
        out_space=HBM,
    )
    return (*(x.reshape(wide, positions) for x in outs), filter_grad)


def solution(mesh):
    block = P("chan", "seq")
    return jax.shard_map(
        on_device,
        mesh=mesh,
        in_specs=(block, block, block, block, P("seq", None)),
        out_specs=(block, block, block, block, P("seq", "chan")),
        check_vma=False,
    )
```
